256 devices in a mesh: row: 16 (over z, core), col: 16 (over x, y).
Axes of the slice: x: 4, y: 4, z: 8, core: 2. Of those that a mesh axis runs over, the one named last changes fastest.
Arguments:
- events: int32 [52, 1024, 4096], P(None, 'row', 'col'), may hold values 0 or 1
- entry_week: int32 [1024, 4096], P('row', 'col'), may hold values from 0 to 25
- exit_week: int32 [1024, 4096], P('row', 'col'), may hold values from 26 to 52
- log_offset: float32 [1024, 4096], P('row', 'col'), may hold values from -3 to 3
- frailty: float32 [1024, 4096], P('row', 'col'), may hold values from -2 to 2
- kappa_sq: float32 [1024, 4096], P('row', 'col'), may hold values from 0.001 to 0.01
- log_rate: float32 [1], replicated, may hold values from -6 to -4
- shape_rate: float32 [1], replicated, may hold values from 0.5 to 2
Outputs:
- newton_step: float32 [1024, 4096], P('row', 'col')
- residual: float32 [1024, 4096], P('row', 'col')
The draws below stay inside these ranges and needn't reach their ends.
All inputs are finite; a program needn't handle non-finite values. No bound on the sum of `events` on one device may be relied on, other than what follows from the above.
Results may differ from the reference program's by a relative error of at most 0.0007.
Values sent between devices are 32-bit elements; how exact they have to be, the bound alone decides.
A program may use at most 128 MiB of HBM per device.

```python
import math
import jax
import jax.numpy as jnp
from jax import lax

WEEKS = 52
ITERS = 8
NR = 1024
NC = 4096


def touch_ends(values, key, low, largest):
    index_at = [jax.random.randint(jax.random.fold_in(key, axis), (), 0, length) for axis, length in enumerate(values.shape)]
    widest = values.shape.index(max(values.shape))
    beside = index_at[:widest] + [(index_at[widest] + 1) % values.shape[widest]] + index_at[widest + 1:]
    return values.at[tuple(index_at)].set(low).at[tuple(beside)].set(largest)


def shard_levels(key, shape, pieces, least, largest):
    def one(position, blocks):
        heights = jax.random.uniform(jax.random.fold_in(jax.random.fold_in(key, 6), position), (blocks,), jnp.float32, least / len(pieces), largest / len(pieces))
        return jnp.repeat(jnp.exp(heights), shape[position] // blocks).reshape((-1,) + (1,) * (len(shape) - position - 1))

    factor_of = one(*pieces[0])
    for cut in pieces[1:]:
        factor_of = factor_of * one(*cut)
    return factor_of


def gaussian(own_key, dims, deviation, most, pieces=(), dtype=jnp.bfloat16):
    drawn = jax.random.normal(own_key, dims, jnp.float32) * deviation
    if len(pieces) > 0:
        drawn = shard_levels(own_key, dims, pieces, -0.22, 0.18) * drawn
    return jnp.clip(drawn, min=-most, max=most).astype(dtype)


def setup_inputs(seed: int = 0) -> dict:
    splits = jax.random.split(jax.random.key(seed), 9)
    return {
        "events": touch_ends((jax.random.randint(splits[0], (WEEKS, NR, NC), 0, 20) < 1).astype(jnp.int32), jax.random.fold_in(splits[0], 1), 0, 1),
        "entry_week": touch_ends(jax.random.randint(splits[1], (NR, NC), 0, 26), jax.random.fold_in(splits[1], 1), 0, 25).astype(jnp.int32),
        "exit_week": touch_ends(jax.random.randint(splits[2], (NR, NC), 26, 53), jax.random.fold_in(splits[2], 1), 26, 52).astype(jnp.int32),
        "log_offset": gaussian(splits[3], (NR, NC), 0.5, 3.0, ((0, 16), (1, 16)), jnp.float32),
        "frailty": gaussian(splits[4], (NR, NC), 0.3, 2.0, ((0, 16), (1, 16)), jnp.float32),
        "kappa_sq": jnp.clip(jnp.exp(math.log(0.01) - 2.30258502 * jax.random.uniform(splits[5], (NR, NC), jnp.float32) ** shard_levels(splits[5], (NR, NC), ((0, 16), (1, 16)), -0.2, 0.2)), 0.001, 0.01),
        "log_rate": jnp.clip(jax.random.uniform(splits[6], (1,), jnp.float32, -6.0, -4.0), -6.0, -4.0),
        "shape_rate": jnp.clip(jax.random.uniform(splits[7], (1,), jnp.float32, 0.5, 2.0), 0.5, 2.0),
    }


TAU = 16.0

def neighbours(field):
    padded = jnp.pad(field, 1)
    return padded[2:, 1:-1] + padded[:-2, 1:-1] + padded[1:-1, 2:] + padded[1:-1, :-2]

def reference(events, entry_week, exit_week, log_offset, frailty, kappa_sq, log_rate, shape_rate):
    week_float = jnp.arange(WEEKS).astype(jnp.float32)
    base = jnp.exp(log_rate[0]) * (jnp.exp(shape_rate[0] * (week_float + 1.0) / WEEKS) - jnp.exp(shape_rate[0] * week_float / WEEKS)) / shape_rate[0]

    def add_week(week, carry):
        count, exposure = carry
        at_risk = ((week >= entry_week) & (week < exit_week)).astype(jnp.float32)
        week_events = lax.dynamic_index_in_dim(events, week, 0, keepdims=False).astype(jnp.float32)
        return (count + at_risk * week_events, exposure + at_risk * base[week])
    zero_field = jnp.zeros(frailty.shape, jnp.float32)
    count, exposure = lax.fori_loop(0, WEEKS, add_week, (zero_field, zero_field))
    weight = exposure * jnp.exp(log_offset + frailty)
    stiff = TAU * (4.0 + kappa_sq)
    gradient = count - weight - (stiff * frailty - TAU * neighbours(frailty))
    full_diag = stiff + weight
    line_diag = 2.0 + kappa_sq + weight / TAU
    lower = jnp.concatenate([jnp.zeros((NR, 1), jnp.float32), -jnp.ones((NR, NC - 1), jnp.float32)], 1)
    upper = jnp.concatenate([-jnp.ones((NR, NC - 1), jnp.float32), jnp.zeros((NR, 1), jnp.float32)], 1)

    def precond(field):
        solved = lax.linalg.tridiagonal_solve(lower, line_diag, upper, (field / TAU)[:, :, None])
        return solved[:, :, 0]

    def apply_a(field):
        return full_diag * field - TAU * neighbours(field)
    newton_step = jnp.zeros_like(gradient)
    residual = gradient
    precond_res = precond(residual)
    direction = precond_res
    norm_now = jnp.sum(residual * precond_res)
    for iteration in range(ITERS):
        image = apply_a(direction)
        step_size = norm_now / jnp.sum(direction * image)
        newton_step = newton_step + step_size * direction
        residual = residual - step_size * image
        if iteration + 1 < ITERS:
            precond_res = precond(residual)
            norm_next = jnp.sum(residual * precond_res)
            direction = precond_res + norm_next / norm_now * direction
            norm_now = norm_next
    return (newton_step, residual)
```

```python
import functools

import jax
import jax.numpy as jnp
from jax import lax
from jax.experimental import pallas as pl
from jax.experimental.pallas import tpu as pltpu
from jax.sharding import PartitionSpec as P


ITERS = 8
TAU = 16.0
MESH = pl.DeviceIdType.MESH
TR, TC = 64, 256
ND = 16
K = 32
GR = 20
EV_PARTS = 4
PIVOT_MIN = 2e-3
f32 = jnp.float32


def iota(shape, dim):
    return lax.broadcasted_iota(jnp.int32, shape, dim)


def seg_transpose(x):
    sub = iota(x.shape, 0) % 4
    seg = iota(x.shape, 1) // 32
    n = x.shape[0]
    out = x
    for d in (1, 2, 3):
        y = jnp.where(sub + d < 4, pltpu.roll(x, n - d, 0), pltpu.roll(x, 4 - d, 0))
        y = pltpu.roll(y, 32 * d, 1)
        out = jnp.where((seg - sub + 4) % 4 == d, y, out)
    return out


def to_groups(tile_of):
    low = iota((8, 128), 0) < 4
    parts = []
    for t in range(TR // 8):
        a, b = tile_of(t, 0), tile_of(t, 1)
        parts.append(jnp.where(low, a, pltpu.roll(b, 4, 0)))
        parts.append(jnp.where(low, pltpu.roll(a, 4, 0), b))
    return seg_transpose(jnp.concatenate(parts, 0))


def kernel(
    mode,
    lr_ref,
    sr_ref,
    ev_hbm,
    en_hbm,
    ex_hbm,
    lo_hbm,
    fr_hbm,
    ka_hbm,
    x_out,
    r_out,
    flag_out,
    ev,
    en,
    ex,
    lo,
    fr,
    ka,
    e_ref,
    hv_rx,
    hh_rx,
    U,
    rx,
    rxv,
    S,
    inv,
    u,
    v,
    pcr,
    Y,
    RHS,
    V,
    RHO,
    AV,
    MK,
    HV,
    GM,
    m1,
    m2,
    g1,
    g2,
    S2,
    OM,
    ORX,
    in_sem,
    hal_send,
    hal_recv,
    rx_send,
    rx_recv,
    rxv_send,
    rxv_recv,
    g_send,
    g_recv,
    o_send,
    o_recv,
):
    i = lax.axis_index("row")
    j = lax.axis_index("col")
    m = j // 2
    up_i, down_i = (i + ND - 1) % ND, (i + 1) % ND
    left_j, right_j = (j + ND - 1) % ND, (j + 1) % ND

    barrier = pltpu.get_barrier_semaphore()

    def hello(a, b):
        pl.semaphore_signal(barrier, inc=1, device_id=(a, b), device_id_type=MESH)

    for d in range(1, ND):
        hello(i, (j + d) % ND)
    for d in range(1, ND):
        hello((i + d) % ND, j)

    @pl.when(j < 2)
    def _():
        for b in range(ND):
            hello(up_i, b)

    @pl.when(j >= ND - 2)
    def _():
        for b in range(ND):
            hello(down_i, b)

    loads = [
        pltpu.make_async_copy(src, dst, in_sem.at[n])
        for n, (src, dst) in enumerate(
            ((fr_hbm, fr), (ex_hbm, ex), (en_hbm, en), (lo_hbm, lo), (ka_hbm, ka))
        )
    ]
    weeks = ev.shape[0] // EV_PARTS
    ev_loads = [
        pltpu.make_async_copy(
            ev_hbm.at[pl.ds(n * weeks, weeks)], ev.at[pl.ds(n * weeks, weeks)], in_sem.at[5 + n]
        )
        for n in range(EV_PARTS)
    ]
    for c in loads + ev_loads:
        c.start()
    for c in loads:
        c.wait()

    rate = jnp.full((1, TC), sr_ref[0], f32)
    scale = jnp.exp(jnp.full((1, TC), lr_ref[0], f32)) / rate
    slope = rate / float(ev.shape[0])
    exposure = scale * (jnp.exp(slope * ex[...].astype(f32)) - jnp.exp(slope * en[...].astype(f32)))
    weight = exposure * jnp.exp(lo[...] + fr[...])
    e_ref[...] = -weight - TAU * (4.0 + ka[...]) * fr[...]
    diag = 2.0 + ka[...] + weight * (1.0 / TAU)

    fill = iota((2, 8, 128), 0) * 0
    for f, value in ((0, 4.0), (1, 0.0)):
        U[f, 0:2] = fill.astype(f32) + value
        U[f, GR - 2 : GR] = fill.astype(f32) + value
    U[0, 2 : GR - 2] = to_groups(
        lambda t, h: diag[8 * t : 8 * t + 8, 128 * h : 128 * h + 128]
    ).reshape(TR // 4, 8, 128)
    part = diag - 2.0
    part = part[:, 0:128] + part[:, 128:256]
    m1[0] = jnp.sum(part.reshape(8, 8, 128), axis=0)

    def field_sends(f):
        out = []
        for d in range(1, ND):
            b = (j + d) % ND
            out.append(
                pltpu.make_async_remote_copy(
                    src_ref=U.at[f, pl.ds(2 * (b // 2), 6)],
                    dst_ref=rx.at[f, j],
                    send_sem=rx_send.at[f],
                    recv_sem=rx_recv.at[f],
                    device_id=(i, b),
                    device_id_type=MESH,
                )
            )
        for first, a, b in (
            (GR - 4, down_i, 0),
            (GR - 4, down_i, 1),
            (2, up_i, ND - 2),
            (2, up_i, ND - 1),
        ):
            out.append(
                pltpu.make_async_remote_copy(
                    src_ref=U.at[f, pl.ds(first, 2)],
                    dst_ref=rxv.at[f, j],
                    send_sem=rxv_send.at[f],
                    recv_sem=rxv_recv.at[f],
                    device_id=(a, b),
                    device_id_type=MESH,
                )
            )
        return out

    def group_sends(src, dst, sem, axis):
        me = j if axis == "col" else i
        return [
            pltpu.make_async_remote_copy(
                src_ref=src,
                dst_ref=dst.at[me],
                send_sem=g_send.at[sem],
                recv_sem=g_recv.at[sem],
                device_id=(i, (j + d) % ND) if axis == "col" else ((i + d) % ND, j),
                device_id_type=MESH,
            )
            for d in range(1, ND)
        ]

    def wait_group(dst, sem):
        whole = pltpu.make_async_remote_copy(
            src_ref=dst.at[pl.ds(0, ND - 1)],
            dst_ref=dst.at[pl.ds(0, ND - 1)],
            send_sem=g_send.at[sem],
            recv_sem=g_recv.at[sem],
            device_id=(i, right_j),
            device_id_type=MESH,
        )
        whole.wait_recv()
        return whole

    def exchange(slot, axis_first):
        first, second = ("row", "col") if axis_first == "row" else ("col", "row")
        me1 = j if first == "col" else i
        me2 = j if second == "col" else i
        for c in group_sends(m1.at[slot], g1.at[slot], 2 * slot, first):
            c.start()
        g1[slot, me1] = m1[slot]
        wait_group(g1.at[slot], 2 * slot)
        m2[slot] = jnp.sum(g1[slot], axis=0)
        for c in group_sends(m2.at[slot], g2.at[slot], 2 * slot + 1, second):
            c.start()
        g2[slot, me2] = m2[slot]
        wait_group(g2.at[slot], 2 * slot + 1)
        return jnp.sum(g2[slot], axis=0)

    pl.semaphore_wait(barrier, 2 * (ND - 1) + 4)

    halos = [
        pltpu.make_async_remote_copy(
            src_ref=src,
            dst_ref=dst,
            send_sem=hal_send.at[n],
            recv_sem=hal_recv.at[n],
            device_id=dev,
            device_id_type=MESH,
        )
        for n, (src, dst, dev) in enumerate(
            (
                (fr.at[pl.ds(TR - 8, 8)], hv_rx.at[0], (down_i, j)),
                (fr.at[pl.ds(0, 8)], hv_rx.at[1], (up_i, j)),
                (fr.at[:, pl.ds(128, 128)], hh_rx.at[0], (i, right_j)),
                (fr.at[:, pl.ds(0, 128)], hh_rx.at[1], (i, left_j)),
            )
        )
    ]
    for c in halos:
        c.start()
    if mode == "fast":
        for c in group_sends(m1.at[0], g1.at[0], 0, "row"):
            c.start()
    for c in field_sends(0):
        c.start()

    en_v, ex_v = en[...], ex[...]
    count = jnp.zeros((TR, TC), jnp.int32)
    for n in range(EV_PARTS):
        ev_loads[n].wait()

        def add_week(w, acc):
            week = w + n * weeks
            at_risk = (week >= en_v) & (week < ex_v)
            return acc + jnp.where(at_risk, ev[week], 0)

        count = lax.fori_loop(0, weeks, add_week, count)
    e_ref[...] = e_ref[...] + count.astype(f32)

    for c in halos:
        c.wait_recv()
    row = iota((TR, 128), 0)
    lane = iota((TR, 128), 1)
    has_up, has_down = jnp.where(i > 0, 1.0, 0.0), jnp.where(i < ND - 1, 1.0, 0.0)
    has_left, has_right = jnp.where(j > 0, 1.0, 0.0), jnp.where(j < ND - 1, 1.0, 0.0)
    halves = []
    for h in (0, 1):
        cols = slice(128 * h, 128 * h + 128)
        here = fr[:, cols]
        above = jnp.where(row == 0, hv_rx[0, 7:8, cols] * has_up, pltpu.roll(here, 1, 0))
        below = jnp.where(row == TR - 1, hv_rx[1, 0:1, cols] * has_down, pltpu.roll(here, TR - 1, 0))
        if h == 0:
            beside_l, beside_r = hh_rx[0] * has_left, fr[:, 128:256]
        else:
            beside_l, beside_r = fr[:, 0:128], hh_rx[1] * has_right
        west = jnp.where(lane == 0, pltpu.roll(beside_l, 1, 1), pltpu.roll(here, 1, 1))
        east = jnp.where(lane == 127, pltpu.roll(beside_r, 127, 1), pltpu.roll(here, 127, 1))
        total = e_ref[:, cols] + TAU * ((below + above) + (east + west))
        halves.append(total * (1.0 / TAU))
    U[1, 2 : GR - 2] = to_groups(lambda t, h: halves[h][8 * t : 8 * t + 8, :]).reshape(TR // 4, 8, 128)
    for c in field_sends(1):
        c.start()

    if mode == "fast":
        g1[0, i] = m1[0]
        wait_group(g1.at[0], 0)
        m2[0] = jnp.sum(g1[0], axis=0)
        for c in group_sends(m2.at[0], g2.at[0], 1, "col"):
            c.start()
        g2[0, j] = m2[0]

    def to_lines(f, dst, outside):
        rx[f, j] = U[f, pl.ds(2 * m, 6)]
        whole = pltpu.make_async_remote_copy(
            src_ref=rx.at[f, pl.ds(0, ND - 1)],
            dst_ref=rx.at[f, pl.ds(0, ND - 1)],
            send_sem=rx_send.at[f],
            recv_sem=rx_recv.at[f],
            device_id=(i, right_j),
            device_id_type=MESH,
        )
        whole.wait_recv()
        beyond = pltpu.make_async_remote_copy(
            src_ref=rxv.at[f],
            dst_ref=rxv.at[f],
            send_sem=rxv_send.at[f],
            recv_sem=rxv_recv.at[f],
            device_id=(i, right_j),
            device_id_type=MESH,
        )

        @pl.when(m == 0)
        def _():
            beyond.wait_recv()
            for b in range(ND):
                rx[f, b, 0:2] = rxv[f, b]

        @pl.when(m == ND // 2 - 1)
        def _():
            beyond.wait_recv()
            for b in range(ND):
                rx[f, b, 4:6] = rxv[f, b]

        for g in range(6):
            S[128 * g : 128 * g + 128] = rx[f, :, g].reshape(128, 128).T
        inside = MK[...] > 0.5
        for k in range(K):
            lines = jnp.concatenate(
                [S[pl.ds(256 * t + k, 8, stride=32), :] for t in range(3)], 0
            )
            dst[k] = jnp.where(inside, lines, outside)

    rows24 = iota((24, 128), 0)
    lanes24 = iota((24, 128), 1)
    lattice_row = TR * i + 8 * (m - 1) + rows24
    MK[...] = jnp.where((lattice_row >= 0) & (lattice_row < TR * ND), 1.0, 0.0)

    to_lines(0, Y, 4.0)

    def after(x):
        return jnp.where(lanes24 == 127, 0.0, pltpu.roll(x, 127, 1))

    def before(x):
        return jnp.where(lanes24 == 0, 0.0, pltpu.roll(x, 1, 1))

    p = 1.0 / Y[0]
    inv[0] = p
    prod = p
    u[0] = prod
    for k in range(1, K - 1):
        p = 1.0 / (Y[k] - p)
        inv[k] = p
        prod = prod * p
        u[k] = prod
    last_u = prod
    q = p
    v[K - 2] = q
    w_u = prod
    for k in range(K - 3, -1, -1):
        p_k = inv[k]
        q = p_k * q
        v[k] = q
        w_u = u[k] + p_k * w_u
        u[k] = w_u
    pivot = 1.0 / (Y[K - 1] - p - after(w_u))
    lo_c = jnp.where(lanes24 == 0, 0.0, last_u) * pivot
    hi_c = after(last_u) * pivot
    pcr[0, 0] = pivot
    for n in range(7):
        s = 1 << n
        d = 1.0 / (1.0 - lo_c * pltpu.roll(hi_c, s, 1) - hi_c * pltpu.roll(lo_c, 128 - s, 1))
        a, b = d * lo_c, d * hi_c
        pcr[n + 1, 0] = d
        pcr[n + 1, 1] = a
        pcr[n + 1, 2] = b
        lo_c = a * pltpu.roll(lo_c, s, 1)
        hi_c = b * pltpu.roll(hi_c, 128 - s, 1)

    to_lines(1, RHS, 0.0)

    def solve(put):
        r = RHS[0]
        f = inv[0] * r
        ends = u[0] * r
        Y[0] = f
        for k in range(1, K - 1):
            r = RHS[k]
            ends = ends + u[k] * r
            f = inv[k] * (r + f)
            Y[k] = f
        x = pcr[0, 0] * (RHS[K - 1] + f + after(ends))
        for n in range(7):
            s = 1 << n
            x = (
                pcr[n + 1, 0] * x
                + pcr[n + 1, 1] * pltpu.roll(x, s, 1)
                + pcr[n + 1, 2] * pltpu.roll(x, 128 - s, 1)
            )
        for k in range(K - 3, -1, -1):
            f = Y[k] + inv[k] * f
            Y[k] = f
        prev = before(x)
        put(K - 1, x)
        for k in range(K - 2, -1, -1):
            put(k, Y[k] + (u[k] * prev + v[k] * x))

    def across(z):
        return MK[...] * (2.0 * z - (pltpu.roll(z, 1, 0) + pltpu.roll(z, 23, 0)))

    own = slice(8, 16)
    sub8 = iota((8, 128), 0)
    lane8 = iota((8, 128), 1)

    if mode == "fast":
        wait_group(g2.at[0], 1)
        mean = jnp.sum(jnp.sum(g2[0], axis=0), axis=(0, 1), keepdims=True) * (
            1.0 / float(TR * TC * ND * ND)
        )
        HV[...] = jnp.broadcast_to(0.5 * mean, (24, 128))
        zero = jnp.zeros((24, 128), f32)
        for n in (0, 1):
            for k in range(K):
                V[n, k] = zero
                RHO[n, k] = zero[own]

        def basis(it, _):
            w = jnp.where(it == 0, 1.0, HV[...])
            twice = jnp.where(it >= 2, 2.0, 1.0)

            def put(k, x):
                vec = twice * (x * w - V[it + 1, k]) - V[it, k]
                rho = twice * (RHS[k, own] * w[own] - RHO[it + 1, k]) - RHO[it, k]
                V[it + 2, k] = vec
                RHO[it + 2, k] = rho
                tv = across(vec)
                AV[it, k] = rho + tv[own]
                RHS[k] = tv

            solve(put)

            def dots(n, _):
                acc_a = [jnp.zeros((8, 128), f32)] * 4
                acc_n = [jnp.zeros((8, 128), f32)] * 4
                for k in range(K):
                    vec = V[it + 2, k, own]
                    acc_a[k % 4] = acc_a[k % 4] + vec * AV[n, k]
                    acc_n[k % 4] = acc_n[k % 4] + vec * RHO[n + 2, k]
                for first, acc in ((0, acc_a), (64, acc_n)):
                    total = jnp.sum((acc[0] + acc[1]) + (acc[2] + acc[3]), axis=0, keepdims=True)
                    GM[pl.ds(first + 56 - 8 * it + n, 1), :] = total
                    GM[pl.ds(first + 56 - 8 * n + it, 1), :] = total
                return 0

            lax.fori_loop(0, it + 1, dots, 0)
            return 0

        lax.fori_loop(0, ITERS, basis, 0)
        m1[1] = jnp.sum(GM[...].T.reshape(16, 8, 128), axis=0)
        total = exchange(1, "col")
        flat = jnp.sum(total, axis=0, keepdims=True)
        mat = pltpu.roll(jnp.broadcast_to(flat, (8, 128)), 0, 1, stride=8, stride_axis=0)
        worst = jnp.full((8, 1), 1.0, f32)
        diag0 = jnp.sum(jnp.where(lane8 == sub8 + 56, mat, 0.0), axis=1, keepdims=True)
        for n in range(ITERS):
            row_n = jnp.sum(jnp.where(sub8 == n, mat, 0.0), axis=0, keepdims=True)
            col_n = jnp.sum(jnp.where(lane8 == 56 + n, mat, 0.0), axis=1, keepdims=True)
            piv = jnp.sum(jnp.where(sub8[:, 0:1] == n, col_n, 0.0), axis=0, keepdims=True)
            first = jnp.sum(jnp.where(sub8[:, 0:1] == n, diag0, 0.0), axis=0, keepdims=True)
            worst = jnp.minimum(worst, jnp.broadcast_to(piv / first, (8, 1)))
            scaled = row_n / piv
            mat = jnp.where(sub8 == n, jnp.broadcast_to(scaled, (8, 128)), mat - col_n * scaled)
        coef = jnp.sum(jnp.where(lane8 == 120, mat, 0.0), axis=1, keepdims=True)
        coef = jnp.broadcast_to(coef, (8, 128))
        odd = j % 2
        coef = coef * jnp.where(odd == 1, -TAU, 1.0)
        base = jnp.where(odd == 1, TAU, 0.0)
        flag_out[...] = jnp.broadcast_to(worst, (8, 128))
        weights = [jnp.broadcast_to(coef[n : n + 1, :], (8, 128)) for n in range(ITERS)]

        @pl.when(odd == 0)
        def _():
            for k in range(K):
                acc = weights[0] * V[2, k, own]
                for n in range(1, ITERS):
                    acc = acc + weights[n] * V[n + 2, k, own]
                S2[pl.ds(k, 8, stride=32), :] = acc

        @pl.when(odd == 1)
        def _():
            for k in range(K):
                acc = weights[0] * AV[0, k]
                for n in range(1, ITERS):
                    acc = acc + weights[n] * AV[n, k]
                S2[pl.ds(k, 8, stride=32), :] = acc + base * RHO[2, k]

    else:
        zero = jnp.zeros((24, 128), f32)
        for n in (3, 4, 5):
            for k in range(K):
                V[n, k] = zero

        def iterate(it, carry):
            gamma_old, alpha_old = carry
            acc = [jnp.zeros((8, 128), f32)] * 4

            def put(k, x):
                r = RHS[k]
                w = MK[...] * r + across(x)
                V[2, k] = x
                V[6, k] = w
                acc[k % 2] = acc[k % 2] + x[own] * r[own]
                acc[2 + k % 2] = acc[2 + k % 2] + x[own] * w[own]

            solve(put)
            gam = jnp.sum(acc[0] + acc[1], axis=0, keepdims=True)
            mu = jnp.sum(acc[2] + acc[3], axis=0, keepdims=True)
            m1[it] = jnp.where(sub8 == 0, gam, jnp.where(sub8 == 1, mu, 0.0))
            total = jnp.sum(exchange(it, "col"), axis=1, keepdims=True)
            gamma = total[0:1]
            mu = total[1:2]
            beta = jnp.where(it == 0, 0.0, gamma / gamma_old)
            alpha = gamma / (mu - beta * gamma / alpha_old)
            for k in range(K):
                p = V[2, k] + beta * V[3, k]
                s = V[6, k] + beta * V[4, k]
                V[3, k] = p
                V[4, k] = s
                V[5, k] = V[5, k] + alpha * p
                RHS[k] = RHS[k] - alpha * s
            return gamma, alpha

        one = jnp.ones((1, 1), f32)
        lax.fori_loop(0, ITERS, iterate, (one, one))
        odd = j % 2
        flag_out[...] = jnp.ones((8, 128), f32)

        @pl.when(odd == 0)
        def _():
            for k in range(K):
                S2[pl.ds(k, 8, stride=32), :] = V[5, k, own]

        @pl.when(odd == 1)
        def _():
            for k in range(K):
                S2[pl.ds(k, 8, stride=32), :] = TAU * RHS[k, own]

    for g in range(2):
        OM[:, g] = S2[128 * g : 128 * g + 128].T.reshape(ND, 8, 128)
    for d in range(1, ND):
        b = (j + d) % ND
        pltpu.make_async_remote_copy(
            src_ref=OM.at[b],
            dst_ref=ORX.at[j],
            send_sem=o_send,
            recv_sem=o_recv,
            device_id=(i, b),
            device_id_type=MESH,
        ).start()
    ORX[j] = OM[j]
    back = pltpu.make_async_remote_copy(
        src_ref=ORX.at[pl.ds(0, ND - 1)],
        dst_ref=ORX.at[pl.ds(0, ND - 1)],
        send_sem=o_send,
        recv_sem=o_recv,
        device_id=(i, right_j),
        device_id_type=MESH,
    )
    back.wait_recv()
    low = iota((8, 128), 0) < 4
    for which, out in ((0, x_out), (1, r_out)):
        groups = jnp.concatenate([ORX[2 * t + which, g] for t in range(TR // 8) for g in range(2)], 0)
        groups = seg_transpose(groups)
        for t in range(TR // 8):
            a = groups[16 * t : 16 * t + 8]
            b = groups[16 * t + 8 : 16 * t + 16]
            out[8 * t : 8 * t + 8, 0:128] = jnp.where(low, a, pltpu.roll(b, 4, 0))
            out[8 * t : 8 * t + 8, 128:256] = jnp.where(low, pltpu.roll(a, 4, 0), b)

    back.wait_send()
    for c in halos:
        c.wait_send()
    for f in (0, 1):
        pltpu.make_async_remote_copy(
            src_ref=rx.at[f, pl.ds(0, ND - 1)],
            dst_ref=rx.at[f, pl.ds(0, ND - 1)],
            send_sem=rx_send.at[f],
            recv_sem=rx_recv.at[f],
            device_id=(i, right_j),
            device_id_type=MESH,
        ).wait_send()
        pltpu.make_async_remote_copy(
            src_ref=rxv.at[f, pl.ds(0, 4)],
            dst_ref=rxv.at[f, pl.ds(0, 4)],
            send_sem=rxv_send.at[f],
            recv_sem=rxv_recv.at[f],
            device_id=(i, right_j),
            device_id_type=MESH,
        ).wait_send()
    for slot in range(2 if mode == "fast" else ITERS):
        for half, dst in ((0, g1), (1, g2)):
            pltpu.make_async_remote_copy(
                src_ref=dst.at[slot, pl.ds(0, ND - 1)],
                dst_ref=dst.at[slot, pl.ds(0, ND - 1)],
                send_sem=g_send.at[2 * slot + half],
                recv_sem=g_recv.at[2 * slot + half],
                device_id=(i, right_j),
                device_id_type=MESH,
            ).wait_send()


def run(mode, events, entry_week, exit_week, log_offset, frailty, kappa_sq, log_rate, shape_rate):
    slots = 2 if mode == "fast" else ITERS
    vm = pltpu.VMEM
    dma = pltpu.SemaphoreType.DMA
    return pl.pallas_call(
        functools.partial(kernel, mode),
        out_shape=(
            jax.ShapeDtypeStruct((TR, TC), f32),
            jax.ShapeDtypeStruct((TR, TC), f32),
            jax.ShapeDtypeStruct((8, 128), f32),
        ),
        in_specs=[pl.BlockSpec(memory_space=pltpu.SMEM)] * 2
        + [pl.BlockSpec(memory_space=pl.ANY)] * 6,
        out_specs=(pl.BlockSpec(memory_space=pltpu.VMEM),) * 3,
        scratch_shapes=[
            vm(events.shape, jnp.int32),
            vm((TR, TC), jnp.int32),
            vm((TR, TC), jnp.int32),
            vm((TR, TC), f32),
            vm((TR, TC), f32),
            vm((TR, TC), f32),
            vm((TR, TC), f32),
            vm((2, 8, TC), f32),
            vm((2, TR, 128), f32),
            vm((2, GR, 8, 128), f32),
            vm((2, ND, 6, 8, 128), f32),
            vm((2, ND, 2, 8, 128), f32),
            vm((768, 128), f32),
            vm((K, 24, 128), f32),
            vm((K, 24, 128), f32),
            vm((K, 24, 128), f32),
            vm((8, 3, 24, 128), f32),
            vm((K, 24, 128), f32),
            vm((K, 24, 128), f32),
            vm((ITERS + 2, K, 24, 128), f32),
            vm((ITERS + 2, K, 8, 128), f32),
            vm((ITERS, K, 8, 128), f32),
            vm((24, 128), f32),
            vm((24, 128), f32),
            vm((128, 128), f32),
            vm((slots, 8, 128), f32),
            vm((slots, 8, 128), f32),
            vm((slots, ND, 8, 128), f32),
            vm((slots, ND, 8, 128), f32),
            vm((256, 128), f32),
            vm((ND, 2, 8, 128), f32),
            vm((ND, 2, 8, 128), f32),
            dma((5 + EV_PARTS,)),
            dma((4,)),
            dma((4,)),
            dma((2,)),
            dma((2,)),
            dma((2,)),
            dma((2,)),
            dma((2 * slots,)),
            dma((2 * slots,)),
            dma,
            dma,
        ],
        compiler_params=pltpu.CompilerParams(
            collective_id=0 if mode == "fast" else 1,
            has_side_effects=True,
            vmem_limit_bytes=40 * 2**20,
        ),
        name="newton_" + mode,
    )(log_rate, shape_rate, events, entry_week, exit_week, log_offset, frailty, kappa_sq)


def per_device(*args):
    step, residual, flag = run("fast", *args)
    return lax.cond(
        flag[0, 0] > PIVOT_MIN,
        lambda: (step, residual),
        lambda: tuple(run("cg", *args)[:2]),
    )


def solution(mesh):
    tile = P("row", "col")
    return jax.shard_map(
        per_device,
        mesh=mesh,
        in_specs=(P(None, "row", "col"), tile, tile, tile, tile, tile, P(), P()),
        out_specs=(tile, tile),
        check_vma=False,
    )
```

```python
import functools

import jax
import jax.numpy as jnp
from jax import lax
from jax.experimental import pallas as pl
from jax.experimental.pallas import tpu as pltpu
from jax.sharding import PartitionSpec as P


ITERS = 8
TAU = 16.0
MESH = pl.DeviceIdType.MESH
TR, TC = 64, 256
ND = 16
K = 32
GR = 20
EV_PARTS = 4
PIVOT_MIN = 2e-3
f32 = jnp.float32


def iota(shape, dim):
    return lax.broadcasted_iota(jnp.int32, shape, dim)


def seg_transpose(x):
    sub = iota(x.shape, 0) % 4
    seg = iota(x.shape, 1) // 32
    n = x.shape[0]
    out = x
    for d in (1, 2, 3):
        y = jnp.where(sub + d < 4, pltpu.roll(x, n - d, 0), pltpu.roll(x, 4 - d, 0))
        y = pltpu.roll(y, 32 * d, 1)
        out = jnp.where((seg - sub + 4) % 4 == d, y, out)
    return out


def to_groups(tile_of):
    low = iota((8, 128), 0) < 4
    parts = []
    for t in range(TR // 8):
        a, b = tile_of(t, 0), tile_of(t, 1)
        parts.append(jnp.where(low, a, pltpu.roll(b, 4, 0)))
        parts.append(jnp.where(low, pltpu.roll(a, 4, 0), b))
    return seg_transpose(jnp.concatenate(parts, 0))


def kernel(
    mode,
    lr_hbm,
    sr_hbm,
    ev_hbm,
    en_hbm,
    ex_hbm,
    lo_hbm,
    fr_hbm,
    ka_hbm,
    x_out,
    r_out,
    flag_out,
    lr_ref,
    sr_ref,
    ev,
    en,
    ex,
    lo,
    fr,
    ka,
    e_ref,
    hv_rx,
    hh_rx,
    U,
    rx,
    rxv,
    S,
    inv,
    u,
    v,
    pcr,
    Y,
    RHS,
    V,
    RHO,
    AV,
    MK,
    HV,
    GM,
    m1,
    m2,
    g1,
    g2,
    S2,
    OM,
    ORX,
    in_sem,
    hal_send,
    hal_recv,
    rx_send,
    rx_recv,
    rxv_send,
    rxv_recv,
    g_send,
    g_recv,
    o_send,
    o_recv,
    s_send,
    s_recv,
):
    i = lax.axis_index("row")
    j = lax.axis_index("col")
    plane, core = i // 2, i % 2
    m = j % 8
    block = 2 * plane + j // 8
    other = i + 1 - 2 * core
    home = block == i
    up_i, down_i = (i + ND - 1) % ND, (i + 1) % ND
    left_j, right_j = (j + ND - 1) % ND, (j + 1) % ND

    barrier = pltpu.get_barrier_semaphore()

    def hello(a, b):
        pl.semaphore_signal(barrier, inc=1, device_id=(a, b), device_id_type=MESH)

    for d in range(1, ND):
        hello(i, (j + d) % ND)
    for d in range(1, ND):
        hello((i + d) % ND, j)
    for d in range(8):
        hello(other, 8 * core + d)

    @pl.when(jnp.logical_not(home))
    def _():
        for b in range(ND):
            hello(other, b)

    ghost_first = (core == 0) & (m == 0)
    ghost_last = (core == 1) & (m == 7)
    ghost_from = (block + jnp.where(core == 0, ND - 1, 1)) % ND
    below_dev = (2 * (down_i // 2), 8 * (down_i % 2))
    above_dev = (2 * (up_i // 2) + 1, 8 * (up_i % 2) + 7)
    below_self = (below_dev[0] == i) & (below_dev[1] == j)
    above_self = (above_dev[0] == i) & (above_dev[1] == j)

    @pl.when(ghost_first | ghost_last)
    def _():
        for b in range(ND):

            @pl.when(jnp.logical_not((ghost_from == i) & (j == b)))
            def _():
                hello(ghost_from, b)

    loads = [
        pltpu.make_async_copy(src, dst, in_sem.at[n])
        for n, (src, dst) in enumerate(
            (
                (fr_hbm, fr),
                (ex_hbm, ex),
                (en_hbm, en),
                (lo_hbm, lo),
                (ka_hbm, ka),
                (lr_hbm, lr_ref),
                (sr_hbm, sr_ref),
            )
        )
    ]
    weeks = ev.shape[0] // EV_PARTS
    ev_loads = [
        pltpu.make_async_copy(
            ev_hbm.at[pl.ds(n * weeks, weeks)], ev.at[pl.ds(n * weeks, weeks)], in_sem.at[7 + n]
        )
        for n in range(EV_PARTS)
    ]
    for c in loads + ev_loads:
        c.start()
    for c in loads:
        c.wait()

    rate = jnp.full((1, TC), sr_ref[0], f32)
    scale = jnp.exp(jnp.full((1, TC), lr_ref[0], f32)) / rate
    slope = rate / float(ev.shape[0])
    exposure = scale * (jnp.exp(slope * ex[...].astype(f32)) - jnp.exp(slope * en[...].astype(f32)))
    weight = exposure * jnp.exp(lo[...] + fr[...])
    e_ref[...] = -weight - TAU * (4.0 + ka[...]) * fr[...]
    diag = 2.0 + ka[...] + weight * (1.0 / TAU)

    fill = iota((2, 8, 128), 0) * 0
    for f, value in ((0, 4.0), (1, 0.0)):
        U[f, 0:2] = fill.astype(f32) + value
        U[f, GR - 2 : GR] = fill.astype(f32) + value
    U[0, 2 : GR - 2] = to_groups(
        lambda t, h: diag[8 * t : 8 * t + 8, 128 * h : 128 * h + 128]
    ).reshape(TR // 4, 8, 128)
    part = diag - 2.0
    part = part[:, 0:128] + part[:, 128:256]
    m1[0] = jnp.sum(part.reshape(8, 8, 128), axis=0)

    def send_field(f):
        for q in (0, 1):
            for d in range(8):
                a = (m + d) % 8
                to = core if q == 0 else 1 - core
                src = U.at[f, pl.ds(2 * a + 3 * to, 3)]

                def start():
                    pltpu.make_async_remote_copy(
                        src_ref=src,
                        dst_ref=rx.at[f, j],
                        send_sem=rx_send.at[f],
                        recv_sem=rx_recv.at[f],
                        device_id=(2 * plane + to, 8 * core + a),
                        device_id_type=MESH,
                    ).start()

                if q == 0 and d == 0:
                    pl.when(jnp.logical_not(home))(start)
                else:
                    start()
        for first, to, here in ((GR - 4, below_dev, below_self), (2, above_dev, above_self)):
            src = U.at[f, pl.ds(first, 2)]

            @pl.when(jnp.logical_not(here))
            def _():
                pltpu.make_async_remote_copy(
                    src_ref=src,
                    dst_ref=rxv.at[f, j],
                    send_sem=rxv_send.at[f],
                    recv_sem=rxv_recv.at[f],
                    device_id=to,
                    device_id_type=MESH,
                ).start()

    def bytes_of(ref, send, recv):
        return pltpu.make_async_remote_copy(
            src_ref=ref,
            dst_ref=ref,
            send_sem=send,
            recv_sem=recv,
            device_id=(i, right_j),
            device_id_type=MESH,
        )

    def one_less(cond, ref, count, send, recv, act):
        @pl.when(cond)
        def _():
            act(bytes_of(ref.at[pl.ds(0, count - 1)], send, recv))

        @pl.when(jnp.logical_not(cond))
        def _():
            act(bytes_of(ref.at[pl.ds(0, count)], send, recv))

    def wait_recv(c):
        c.wait_recv()

    def wait_send(c):
        c.wait_send()

    def group_sends(src, dst, sem, axis):
        if axis == "col":
            me, to = j, [(i, (j + d) % ND) for d in range(1, ND)]
        elif axis == "row":
            me, to = i, [((i + d) % ND, j) for d in range(1, ND)]
        else:
            me, to = plane, [((i + 2 * d) % ND, j) for d in range(1, ND // 2)]
        for dev in to:
            pltpu.make_async_remote_copy(
                src_ref=src,
                dst_ref=dst.at[me],
                send_sem=g_send.at[sem],
                recv_sem=g_recv.at[sem],
                device_id=dev,
                device_id_type=MESH,
            ).start()
        dst[me] = src[...]

    def group_bytes(dst, sem, count):
        return bytes_of(dst.at[pl.ds(0, count - 1)], g_send.at[sem], g_recv.at[sem])

    def exchange(slot):
        group_sends(m1.at[slot], g1.at[slot], 2 * slot, "col")
        group_bytes(g1.at[slot], 2 * slot, ND).wait_recv()
        m2[slot] = jnp.sum(g1[slot], axis=0)
        group_sends(m2.at[slot], g2.at[slot], 2 * slot + 1, "plane")
        group_bytes(g2.at[slot], 2 * slot + 1, ND // 2).wait_recv()
        return jnp.sum(g2[slot, 0 : ND // 2], axis=0)

    greeted = 2 * (ND - 1) + 8 + 2
    greeted = greeted + jnp.where(home, 0, ND)
    greeted = greeted - jnp.where(below_self, 1, 0) - jnp.where(above_self, 1, 0)
    pl.semaphore_wait(barrier, greeted)

    halos = [
        pltpu.make_async_remote_copy(
            src_ref=src,
            dst_ref=dst,
            send_sem=hal_send.at[n],
            recv_sem=hal_recv.at[n],
            device_id=dev,
            device_id_type=MESH,
        )
        for n, (src, dst, dev) in enumerate(
            (
                (fr.at[pl.ds(TR - 8, 8)], hv_rx.at[0], (down_i, j)),
                (fr.at[pl.ds(0, 8)], hv_rx.at[1], (up_i, j)),
                (fr.at[:, pl.ds(128, 128)], hh_rx.at[0], (i, right_j)),
                (fr.at[:, pl.ds(0, 128)], hh_rx.at[1], (i, left_j)),
            )
        )
    ]
    for c in halos:
        c.start()
    if mode == "fast":
        group_sends(m1.at[0], g1.at[0], 0, "row")
    send_field(0)

    en_v, ex_v = en[...], ex[...]
    count = jnp.zeros((TR, TC), jnp.int32)
    for n in range(EV_PARTS):
        ev_loads[n].wait()

        def add_week(w, acc):
            week = w + n * weeks
            at_risk = (week >= en_v) & (week < ex_v)
            return acc + jnp.where(at_risk, ev[week], 0)

        count = lax.fori_loop(0, weeks, add_week, count)
    e_ref[...] = e_ref[...] + count.astype(f32)

    for c in halos:
        c.wait_recv()
    row = iota((TR, 128), 0)
    lane = iota((TR, 128), 1)
    has_up, has_down = jnp.where(i > 0, 1.0, 0.0), jnp.where(i < ND - 1, 1.0, 0.0)
    has_left, has_right = jnp.where(j > 0, 1.0, 0.0), jnp.where(j < ND - 1, 1.0, 0.0)
    halves = []
    for h in (0, 1):
        cols = slice(128 * h, 128 * h + 128)
        here = fr[:, cols]
        above = jnp.where(row == 0, hv_rx[0, 7:8, cols] * has_up, pltpu.roll(here, 1, 0))
        below = jnp.where(row == TR - 1, hv_rx[1, 0:1, cols] * has_down, pltpu.roll(here, TR - 1, 0))
        if h == 0:
            beside_l, beside_r = hh_rx[0] * has_left, fr[:, 128:256]
        else:
            beside_l, beside_r = fr[:, 0:128], hh_rx[1] * has_right
        west = jnp.where(lane == 0, pltpu.roll(beside_l, 1, 1), pltpu.roll(here, 1, 1))
        east = jnp.where(lane == 127, pltpu.roll(beside_r, 127, 1), pltpu.roll(here, 127, 1))
        total = e_ref[:, cols] + TAU * ((below + above) + (east + west))
        halves.append(total * (1.0 / TAU))
    U[1, 2 : GR - 2] = to_groups(lambda t, h: halves[h][8 * t : 8 * t + 8, :]).reshape(TR // 4, 8, 128)
    send_field(1)

    if mode == "fast":
        group_bytes(g1.at[0], 0, ND).wait_recv()
        m2[0] = jnp.sum(g1[0], axis=0)
        group_sends(m2.at[0], g2.at[0], 1, "col")

    def to_lines(f, dst, outside):
        @pl.when(home)
        def _():
            rx[f, j] = U[f, pl.ds(2 * m + 3 * core, 3)]

        one_less(home, rx.at[f], ND, rx_send.at[f], rx_recv.at[f], wait_recv)

        def ghosts(first, own_first, cond):
            @pl.when(cond)
            def _():
                self_too = ghost_from == i

                @pl.when(self_too)
                def _():
                    rxv[f, j] = U[f, pl.ds(own_first, 2)]

                one_less(self_too, rxv.at[f], ND, rxv_send.at[f], rxv_recv.at[f], wait_recv)
                for b in range(ND):
                    rx[f, b, first : first + 2] = rxv[f, b]

        ghosts(0, GR - 4, ghost_first)
        ghosts(1, 2, ghost_last)
        for g in range(3):
            at = pl.ds(384 * core + 128 * g, 128)
            S[f, at] = rx[f, :, g].reshape(128, 128).T
            pltpu.make_async_remote_copy(
                src_ref=S.at[f, at],
                dst_ref=S.at[f, at],
                send_sem=s_send.at[f],
                recv_sem=s_recv.at[f],
                device_id=(other, j),
                device_id_type=MESH,
            ).start()
        bytes_of(S.at[f, pl.ds(0, 384)], s_send.at[f], s_recv.at[f]).wait_recv()
        inside = MK[...] > 0.5
        for k in range(K):
            lines = jnp.concatenate(
                [S[f, pl.ds(256 * t + k, 8, stride=32), :] for t in range(3)], 0
            )
            dst[k] = jnp.where(inside, lines, outside)

    rows24 = iota((24, 128), 0)
    lanes24 = iota((24, 128), 1)
    lattice_row = 2 * TR * plane + 8 * (j - 1) + rows24
    MK[...] = jnp.where((lattice_row >= 0) & (lattice_row < TR * ND), 1.0, 0.0)

    to_lines(0, Y, 4.0)

    def after(x):
        return jnp.where(lanes24 == 127, 0.0, pltpu.roll(x, 127, 1))

    def before(x):
        return jnp.where(lanes24 == 0, 0.0, pltpu.roll(x, 1, 1))

    p = 1.0 / Y[0]
    inv[0] = p
    prod = p
    u[0] = prod
    for k in range(1, K - 1):
        p = 1.0 / (Y[k] - p)
        inv[k] = p
        prod = prod * p
        u[k] = prod
    last_u = prod
    q = p
    v[K - 2] = q
    w_u = prod
    for k in range(K - 3, -1, -1):
        p_k = inv[k]
        q = p_k * q
        v[k] = q
        w_u = u[k] + p_k * w_u
        u[k] = w_u
    pivot = 1.0 / (Y[K - 1] - p - after(w_u))
    lo_c = jnp.where(lanes24 == 0, 0.0, last_u) * pivot
    hi_c = after(last_u) * pivot
    pcr[0, 0] = pivot
    for n in range(7):
        s = 1 << n
        d = 1.0 / (1.0 - lo_c * pltpu.roll(hi_c, s, 1) - hi_c * pltpu.roll(lo_c, 128 - s, 1))
        a, b = d * lo_c, d * hi_c
        pcr[n + 1, 0] = d
        pcr[n + 1, 1] = a
        pcr[n + 1, 2] = b
        lo_c = a * pltpu.roll(lo_c, s, 1)
        hi_c = b * pltpu.roll(hi_c, 128 - s, 1)

    to_lines(1, RHS, 0.0)

    def solve(put):
        r = RHS[0]
        f = inv[0] * r
        ends = u[0] * r
        Y[0] = f
        for k in range(1, K - 1):
            r = RHS[k]
            ends = ends + u[k] * r
            f = inv[k] * (r + f)
            Y[k] = f
        x = pcr[0, 0] * (RHS[K - 1] + f + after(ends))
        for n in range(7):
            s = 1 << n
            x = (
                pcr[n + 1, 0] * x
                + pcr[n + 1, 1] * pltpu.roll(x, s, 1)
                + pcr[n + 1, 2] * pltpu.roll(x, 128 - s, 1)
            )
        for k in range(K - 3, -1, -1):
            f = Y[k] + inv[k] * f
            Y[k] = f
        prev = before(x)
        put(K - 1, x)
        for k in range(K - 2, -1, -1):
            put(k, Y[k] + (u[k] * prev + v[k] * x))

    def across(z):
        return MK[...] * (2.0 * z - (pltpu.roll(z, 1, 0) + pltpu.roll(z, 23, 0)))

    own = slice(8, 16)
    sub8 = iota((8, 128), 0)
    lane8 = iota((8, 128), 1)

    if mode == "fast":
        group_bytes(g2.at[0], 1, ND).wait_recv()
        mean = jnp.sum(jnp.sum(g2[0], axis=0), axis=(0, 1), keepdims=True) * (
            1.0 / float(TR * TC * ND * ND)
        )
        HV[...] = jnp.broadcast_to(0.5 * mean, (24, 128))
        zero = jnp.zeros((24, 128), f32)
        for n in (0, 1):
            for k in range(K):
                V[n, k] = zero
                RHO[n, k] = zero[own]

        def basis(it, _):
            w = jnp.where(it == 0, 1.0, HV[...])
            twice = jnp.where(it >= 2, 2.0, 1.0)

            def put(k, x):
                vec = twice * (x * w - V[it + 1, k]) - V[it, k]
                rho = twice * (RHS[k, own] * w[own] - RHO[it + 1, k]) - RHO[it, k]
                V[it + 2, k] = vec
                RHO[it + 2, k] = rho
                tv = across(vec)
                AV[it, k] = rho + tv[own]
                RHS[k] = tv

            solve(put)

            def dots(n, _):
                acc_a = [jnp.zeros((8, 128), f32)] * 4
                acc_n = [jnp.zeros((8, 128), f32)] * 4
                for k in range(K):
                    vec = V[it + 2, k, own]
                    acc_a[k % 4] = acc_a[k % 4] + vec * AV[n, k]
                    acc_n[k % 4] = acc_n[k % 4] + vec * RHO[n + 2, k]
                for first, acc in ((0, acc_a), (64, acc_n)):
                    total = jnp.sum((acc[0] + acc[1]) + (acc[2] + acc[3]), axis=0, keepdims=True)
                    GM[pl.ds(first + 56 - 8 * it + n, 1), :] = total
                    GM[pl.ds(first + 56 - 8 * n + it, 1), :] = total
                return 0

            lax.fori_loop(0, it + 1, dots, 0)
            return 0

        lax.fori_loop(0, ITERS, basis, 0)
        m1[1] = jnp.sum(GM[...].T.reshape(16, 8, 128), axis=0)
        total = exchange(1)
        flat = jnp.sum(total, axis=0, keepdims=True)
        mat = pltpu.roll(jnp.broadcast_to(flat, (8, 128)), 0, 1, stride=8, stride_axis=0)
        worst = jnp.full((8, 1), 1.0, f32)
        diag0 = jnp.sum(jnp.where(lane8 == sub8 + 56, mat, 0.0), axis=1, keepdims=True)
        for n in range(ITERS):
            row_n = jnp.sum(jnp.where(sub8 == n, mat, 0.0), axis=0, keepdims=True)
            col_n = jnp.sum(jnp.where(lane8 == 56 + n, mat, 0.0), axis=1, keepdims=True)
            piv = jnp.sum(jnp.where(sub8[:, 0:1] == n, col_n, 0.0), axis=0, keepdims=True)
            first = jnp.sum(jnp.where(sub8[:, 0:1] == n, diag0, 0.0), axis=0, keepdims=True)
            worst = jnp.minimum(worst, jnp.broadcast_to(piv / first, (8, 1)))
            scaled = row_n / piv
            mat = jnp.where(sub8 == n, jnp.broadcast_to(scaled, (8, 128)), mat - col_n * scaled)
        coef = jnp.sum(jnp.where(lane8 == 120, mat, 0.0), axis=1, keepdims=True)
        coef = jnp.broadcast_to(coef, (8, 128))
        odd = core
        coef = coef * jnp.where(odd == 1, -TAU, 1.0)
        base = jnp.where(odd == 1, TAU, 0.0)
        flag_out[0] = jnp.where(jnp.min(worst) > PIVOT_MIN, 1, 0)
        weights = [jnp.broadcast_to(coef[n : n + 1, :], (8, 128)) for n in range(ITERS)]

        @pl.when(odd == 0)
        def _():
            for k in range(K):
                acc = weights[0] * V[2, k, own]
                for n in range(1, ITERS):
                    acc = acc + weights[n] * V[n + 2, k, own]
                S2[pl.ds(k, 8, stride=32), :] = acc

        @pl.when(odd == 1)
        def _():
            for k in range(K):
                acc = weights[0] * AV[0, k]
                for n in range(1, ITERS):
                    acc = acc + weights[n] * AV[n, k]
                S2[pl.ds(k, 8, stride=32), :] = acc + base * RHO[2, k]

    else:
        zero = jnp.zeros((24, 128), f32)
        for n in (3, 4, 5):
            for k in range(K):
                V[n, k] = zero

        def iterate(it, carry):
            gamma_old, alpha_old = carry
            acc = [jnp.zeros((8, 128), f32)] * 4

            def put(k, x):
                r = RHS[k]
                w = MK[...] * r + across(x)
                V[2, k] = x
                V[6, k] = w
                acc[k % 2] = acc[k % 2] + x[own] * r[own]
                acc[2 + k % 2] = acc[2 + k % 2] + x[own] * w[own]

            solve(put)
            gam = jnp.sum(acc[0] + acc[1], axis=0, keepdims=True)
            mu = jnp.sum(acc[2] + acc[3], axis=0, keepdims=True)
            m1[it] = jnp.where(sub8 == 0, gam, jnp.where(sub8 == 1, mu, 0.0))
            total = jnp.sum(exchange(it), axis=1, keepdims=True)
            gamma = total[0:1]
            mu = total[1:2]
            beta = jnp.where(it == 0, 0.0, gamma / gamma_old)
            alpha = gamma / (mu - beta * gamma / alpha_old)
            for k in range(K):
                p = V[2, k] + beta * V[3, k]
                s = V[6, k] + beta * V[4, k]
                V[3, k] = p
                V[4, k] = s
                V[5, k] = V[5, k] + alpha * p
                RHS[k] = RHS[k] - alpha * s
            return gamma, alpha

        one = jnp.ones((1, 1), f32)
        lax.fori_loop(0, ITERS, iterate, (one, one))
        odd = core
        flag_out[0] = 1

        @pl.when(odd == 0)
        def _():
            for k in range(K):
                S2[pl.ds(k, 8, stride=32), :] = V[5, k, own]

        @pl.when(odd == 1)
        def _():
            for k in range(K):
                S2[pl.ds(k, 8, stride=32), :] = TAU * RHS[k, own]

    for g in range(2):
        OM[:, g] = S2[128 * g : 128 * g + 128].T.reshape(ND, 8, 128)
    slot = 2 * m + core
    for d in range(ND):
        b = (j + d) % ND

        def start():
            pltpu.make_async_remote_copy(
                src_ref=OM.at[b],
                dst_ref=ORX.at[slot],
                send_sem=o_send,
                recv_sem=o_recv,
                device_id=(block, b),
                device_id_type=MESH,
            ).start()

        if d == 0:
            pl.when(jnp.logical_not(home))(start)
        else:
            start()

    @pl.when(home)
    def _():
        ORX[slot] = OM[j]

    one_less(home, ORX, ND, o_send, o_recv, wait_recv)
    low = iota((8, 128), 0) < 4
    for which, out in ((0, x_out), (1, r_out)):
        groups = jnp.concatenate([ORX[2 * t + which, g] for t in range(TR // 8) for g in range(2)], 0)
        groups = seg_transpose(groups)
        for t in range(TR // 8):
            a = groups[16 * t : 16 * t + 8]
            b = groups[16 * t + 8 : 16 * t + 16]
            out[8 * t : 8 * t + 8, 0:128] = jnp.where(low, a, pltpu.roll(b, 4, 0))
            out[8 * t : 8 * t + 8, 128:256] = jnp.where(low, pltpu.roll(a, 4, 0), b)

    one_less(home, ORX, ND, o_send, o_recv, wait_send)
    for c in halos:
        c.wait_send()
    for f in (0, 1):
        one_less(home, rx.at[f], ND, rx_send.at[f], rx_recv.at[f], wait_send)
        bytes_of(S.at[f, pl.ds(0, 384)], s_send.at[f], s_recv.at[f]).wait_send()
        one_less(
            below_self | above_self, rxv.at[f], 2, rxv_send.at[f], rxv_recv.at[f], wait_send
        )
    for slot in range(2 if mode == "fast" else ITERS):
        first = slot == 0 and mode == "fast"
        group_bytes(g1.at[slot], 2 * slot, ND).wait_send()
        group_bytes(g2.at[slot], 2 * slot + 1, ND if first else ND // 2).wait_send()


def run(mode, events, entry_week, exit_week, log_offset, frailty, kappa_sq, log_rate, shape_rate):
    slots = 2 if mode == "fast" else ITERS
    vm = pltpu.VMEM
    dma = pltpu.SemaphoreType.DMA
    return pl.pallas_call(
        functools.partial(kernel, mode),
        out_shape=(
            jax.ShapeDtypeStruct((TR, TC), f32),
            jax.ShapeDtypeStruct((TR, TC), f32),
            jax.ShapeDtypeStruct((1,), jnp.int32),
        ),
        in_specs=[pl.BlockSpec(memory_space=pltpu.HBM)] * 8,
        out_specs=(
            pl.BlockSpec(memory_space=pltpu.VMEM),
            pl.BlockSpec(memory_space=pltpu.VMEM),
            pl.BlockSpec(memory_space=pltpu.SMEM),
        ),
        scratch_shapes=[
            pltpu.SMEM((1,), f32),
            pltpu.SMEM((1,), f32),
            vm(events.shape, jnp.int32),
            vm((TR, TC), jnp.int32),
            vm((TR, TC), jnp.int32),
            vm((TR, TC), f32),
            vm((TR, TC), f32),
            vm((TR, TC), f32),
            vm((TR, TC), f32),
            vm((2, 8, TC), f32),
            vm((2, TR, 128), f32),
            vm((2, GR, 8, 128), f32),
            vm((2, ND, 3, 8, 128), f32),
            vm((2, ND, 2, 8, 128), f32),
            vm((2, 768, 128), f32),
            vm((K, 24, 128), f32),
            vm((K, 24, 128), f32),
            vm((K, 24, 128), f32),
            vm((8, 3, 24, 128), f32),
            vm((K, 24, 128), f32),
            vm((K, 24, 128), f32),
            vm((ITERS + 2, K, 24, 128), f32),
            vm((ITERS + 2, K, 8, 128), f32),
            vm((ITERS, K, 8, 128), f32),
            vm((24, 128), f32),
            vm((24, 128), f32),
            vm((128, 128), f32),
            vm((slots, 8, 128), f32),
            vm((slots, 8, 128), f32),
            vm((slots, ND, 8, 128), f32),
            vm((slots, ND, 8, 128), f32),
            vm((256, 128), f32),
            vm((ND, 2, 8, 128), f32),
            vm((ND, 2, 8, 128), f32),
            dma((7 + EV_PARTS,)),
            dma((4,)),
            dma((4,)),
            dma((2,)),
            dma((2,)),
            dma((2,)),
            dma((2,)),
            dma((2 * slots,)),
            dma((2 * slots,)),
            dma,
            dma,
            dma((2,)),
            dma((2,)),
        ],
        compiler_params=pltpu.CompilerParams(
            collective_id=0 if mode == "fast" else 1,
            has_side_effects=True,
            vmem_limit_bytes=40 * 2**20,
        ),
        name="newton_" + mode,
    )(log_rate, shape_rate, events, entry_week, exit_week, log_offset, frailty, kappa_sq)


def per_device(*args):
    step, residual, flag = run("fast", *args)
    return lax.cond(
        flag[0] > 0,
        lambda: (step, residual),
        lambda: tuple(run("cg", *args)[:2]),
    )


def solution(mesh):
    tile = P("row", "col")
    return jax.shard_map(
        per_device,
        mesh=mesh,
        in_specs=(P(None, "row", "col"), tile, tile, tile, tile, tile, P(), P()),
        out_specs=(tile, tile),
        check_vma=False,
    )
```

```python
import functools

import jax
import jax.numpy as jnp
from jax import lax
from jax.experimental import pallas as pl
from jax.experimental.pallas import tpu as pltpu
from jax.sharding import PartitionSpec as P


ITERS = 8
TAU = 16.0
MESH = pl.DeviceIdType.MESH
TR, TC = 64, 256
ND = 16
K = 32
GR = 20
EV_PARTS = 4
PIVOT_MIN = 2e-3
W = 2
f32 = jnp.float32


def iota(shape, dim):
    return lax.broadcasted_iota(jnp.int32, shape, dim)


def turn(x, by):
    by = by % 128
    return pltpu.roll(x, by, 1) if by else x


def compose(later, earlier):
    out = {}
    for o, x in later.items():
        for q, y in earlier.items():
            term = x * turn(y, o)
            at = (o + q) % 128
            out[at] = out[at] + term if at in out else term
    return out


def seg_transpose(x):
    sub = iota(x.shape, 0) % 4
    seg = iota(x.shape, 1) // 32
    n = x.shape[0]
    out = x
    for d in (1, 2, 3):
        y = jnp.where(sub + d < 4, pltpu.roll(x, n - d, 0), pltpu.roll(x, 4 - d, 0))
        y = pltpu.roll(y, 32 * d, 1)
        out = jnp.where((seg - sub + 4) % 4 == d, y, out)
    return out


def to_groups(tile_of):
    low = iota((8, 128), 0) < 4
    parts = []
    for t in range(TR // 8):
        a, b = tile_of(t, 0), tile_of(t, 1)
        parts.append(jnp.where(low, a, pltpu.roll(b, 4, 0)))
        parts.append(jnp.where(low, pltpu.roll(a, 4, 0), b))
    return seg_transpose(jnp.concatenate(parts, 0))


def kernel(
    mode,
    lr_hbm,
    sr_hbm,
    ev_hbm,
    en_hbm,
    ex_hbm,
    lo_hbm,
    fr_hbm,
    ka_hbm,
    x_out,
    r_out,
    flag_out,
    lr_ref,
    sr_ref,
    ev,
    en,
    ex,
    lo,
    fr,
    ka,
    e_ref,
    hv_rx,
    hh_tx,
    hh_rx,
    U,
    rx,
    rxv,
    S,
    inv,
    u,
    v,
    pcr,
    Y,
    RHS,
    V,
    RHO,
    AV,
    MK,
    HV,
    GM,
    m1,
    m2,
    g1,
    g2,
    S2,
    OM,
    ORX,
    in_sem,
    hal_send,
    hal_recv,
    rx_send,
    rx_recv,
    rxv_send,
    rxv_recv,
    g_send,
    g_recv,
    o_send,
    o_recv,
    s_send,
    s_recv,
):
    i = lax.axis_index("row")
    j = lax.axis_index("col")
    plane, core = i // 2, i % 2
    m = j % 8
    block = 2 * plane + j // 8
    other = i + 1 - 2 * core
    home = block == i
    up_i, down_i = (i + ND - 1) % ND, (i + 1) % ND
    left_j, right_j = (j + ND - 1) % ND, (j + 1) % ND

    barrier = pltpu.get_barrier_semaphore()

    def hello(a, b):
        pl.semaphore_signal(barrier, inc=1, device_id=(a, b), device_id_type=MESH)

    for d in range(1, ND):
        hello(i, (j + d) % ND)
    for d in range(1, ND):
        hello((i + d) % ND, j)
    for d in range(8):
        hello(other, 8 * core + d)

    @pl.when(jnp.logical_not(home))
    def _():
        for b in range(ND):
            hello(other, b)

    ghost_first = (core == 0) & (m == 0)
    ghost_last = (core == 1) & (m == 7)
    ghost_from = (block + jnp.where(core == 0, ND - 1, 1)) % ND
    below_dev = (2 * (down_i // 2), 8 * (down_i % 2))
    above_dev = (2 * (up_i // 2) + 1, 8 * (up_i % 2) + 7)
    below_self = (below_dev[0] == i) & (below_dev[1] == j)
    above_self = (above_dev[0] == i) & (above_dev[1] == j)

    @pl.when(ghost_first | ghost_last)
    def _():
        for b in range(ND):

            @pl.when(jnp.logical_not((ghost_from == i) & (j == b)))
            def _():
                hello(ghost_from, b)

    loads = [
        pltpu.make_async_copy(src, dst, in_sem.at[n])
        for n, (src, dst) in enumerate(
            (
                (fr_hbm, fr),
                (ex_hbm, ex),
                (en_hbm, en),
                (lo_hbm, lo),
                (ka_hbm, ka),
                (lr_hbm, lr_ref),
                (sr_hbm, sr_ref),
            )
        )
    ]
    weeks = ev.shape[0] // EV_PARTS
    ev_loads = [
        pltpu.make_async_copy(
            ev_hbm.at[pl.ds(n * weeks, weeks)], ev.at[pl.ds(n * weeks, weeks)], in_sem.at[7 + n]
        )
        for n in range(EV_PARTS)
    ]
    for c in loads + ev_loads:
        c.start()
    for c in loads:
        c.wait()

    flipped = jnp.concatenate([fr[:, 128:256], fr[:, 0:128]], 0).T
    hh_tx[0] = flipped[120:128]
    hh_tx[1] = flipped[0:8]
    rate = jnp.full((1, TC), sr_ref[0], f32)
    scale = jnp.exp(jnp.full((1, TC), lr_ref[0], f32)) / rate
    slope = rate / float(ev.shape[0])
    exposure = scale * (jnp.exp(slope * ex[...].astype(f32)) - jnp.exp(slope * en[...].astype(f32)))
    weight = exposure * jnp.exp(lo[...] + fr[...])
    e_ref[...] = -weight - TAU * (4.0 + ka[...]) * fr[...]
    diag = 2.0 + ka[...] + weight * (1.0 / TAU)

    fill = iota((2, 8, 128), 0) * 0
    for f, value in ((0, 4.0), (1, 0.0)):
        U[f, 0:2] = fill.astype(f32) + value
        U[f, GR - 2 : GR] = fill.astype(f32) + value
    U[0, 2 : GR - 2] = to_groups(
        lambda t, h: diag[8 * t : 8 * t + 8, 128 * h : 128 * h + 128]
    ).reshape(TR // 4, 8, 128)
    part = diag - 2.0
    part = part[:, 0:128] + part[:, 128:256]
    part = jnp.sum(part, axis=0, keepdims=True)
    m1[0] = jnp.where(iota((W, 128), 0) == 0, part, 0.0)

    def send_field(f):
        for q in (0, 1):
            for d in range(8):
                a = (m + d) % 8
                to = core if q == 0 else 1 - core
                src = U.at[f, pl.ds(2 * a + 3 * to, 3)]

                def start():
                    pltpu.make_async_remote_copy(
                        src_ref=src,
                        dst_ref=rx.at[f, j],
                        send_sem=rx_send.at[f],
                        recv_sem=rx_recv.at[f],
                        device_id=(2 * plane + to, 8 * core + a),
                        device_id_type=MESH,
                    ).start()

                if q == 0 and d == 0:
                    pl.when(jnp.logical_not(home))(start)
                else:
                    start()
        for first, to, here in ((GR - 4, below_dev, below_self), (2, above_dev, above_self)):
            src = U.at[f, pl.ds(first, 2)]

            @pl.when(jnp.logical_not(here))
            def _():
                pltpu.make_async_remote_copy(
                    src_ref=src,
                    dst_ref=rxv.at[f, j],
                    send_sem=rxv_send.at[f],
                    recv_sem=rxv_recv.at[f],
                    device_id=to,
                    device_id_type=MESH,
                ).start()

    def bytes_of(ref, send, recv):
        return pltpu.make_async_remote_copy(
            src_ref=ref,
            dst_ref=ref,
            send_sem=send,
            recv_sem=recv,
            device_id=(i, right_j),
            device_id_type=MESH,
        )

    def one_less(cond, ref, count, send, recv, act):
        @pl.when(cond)
        def _():
            act(bytes_of(ref.at[pl.ds(0, count - 1)], send, recv))

        @pl.when(jnp.logical_not(cond))
        def _():
            act(bytes_of(ref.at[pl.ds(0, count)], send, recv))

    def wait_recv(c):
        c.wait_recv()

    def wait_send(c):
        c.wait_send()

    def group_sends(src, dst, sem, axis):
        if axis == "col":
            me, to = j, [(i, (j + d) % ND) for d in range(1, ND)]
        elif axis == "row":
            me, to = i, [((i + d) % ND, j) for d in range(1, ND)]
        else:
            me, to = plane, [((i + 2 * d) % ND, j) for d in range(1, ND // 2)]
        for dev in to:
            pltpu.make_async_remote_copy(
                src_ref=src,
                dst_ref=dst.at[me],
                send_sem=g_send.at[sem],
                recv_sem=g_recv.at[sem],
                device_id=dev,
                device_id_type=MESH,
            ).start()
        dst[me] = src[...]

    def group_bytes(dst, sem, count):
        return bytes_of(dst.at[pl.ds(0, count - 1)], g_send.at[sem], g_recv.at[sem])

    def exchange(slot):
        group_sends(m1.at[slot], g1.at[slot], 2 * slot, "col")
        group_bytes(g1.at[slot], 2 * slot, ND).wait_recv()
        m2[slot] = jnp.sum(g1[slot], axis=0)
        group_sends(m2.at[slot], g2.at[slot], 2 * slot + 1, "plane")
        group_bytes(g2.at[slot], 2 * slot + 1, ND // 2).wait_recv()
        return jnp.sum(g2[slot, 0 : ND // 2], axis=0)

    greeted = 2 * (ND - 1) + 8 + 2
    greeted = greeted + jnp.where(home, 0, ND)
    greeted = greeted - jnp.where(below_self, 1, 0) - jnp.where(above_self, 1, 0)
    pl.semaphore_wait(barrier, greeted)

    halos = [
        pltpu.make_async_remote_copy(
            src_ref=src,
            dst_ref=dst,
            send_sem=hal_send.at[n],
            recv_sem=hal_recv.at[n],
            device_id=dev,
            device_id_type=MESH,
        )
        for n, (src, dst, dev) in enumerate(
            (
                (fr.at[pl.ds(TR - 8, 8)], hv_rx.at[0], (down_i, j)),
                (fr.at[pl.ds(0, 8)], hv_rx.at[1], (up_i, j)),
                (hh_tx.at[0], hh_rx.at[0], (i, right_j)),
                (hh_tx.at[1], hh_rx.at[1], (i, left_j)),
            )
        )
    ]
    for c in halos:
        c.start()
    if mode == "fast":
        group_sends(m1.at[0], g1.at[0], 0, "row")
    send_field(0)

    en_v, ex_v = en[...], ex[...]
    count = jnp.zeros((TR, TC), jnp.int32)
    for n in range(EV_PARTS):
        ev_loads[n].wait()

        def add_week(w, acc):
            week = w + n * weeks
            at_risk = (week >= en_v) & (week < ex_v)
            return acc + jnp.where(at_risk, ev[week], 0)

        count = lax.fori_loop(0, weeks, add_week, count)
    e_ref[...] = e_ref[...] + count.astype(f32)

    for c in halos:
        c.wait_recv()
    row = iota((TR, 128), 0)
    lane = iota((TR, 128), 1)
    has_up, has_down = jnp.where(i > 0, 1.0, 0.0), jnp.where(i < ND - 1, 1.0, 0.0)
    has_left, has_right = jnp.where(j > 0, 1.0, 0.0), jnp.where(j < ND - 1, 1.0, 0.0)
    lane1 = iota((1, 128), 1)
    edges = jnp.where(lane1 < TR, hh_rx[0, 7:8] * has_left, hh_rx[1, 0:1] * has_right)
    edges = jnp.broadcast_to(edges, (128, 128)).T
    halves = []
    for h in (0, 1):
        cols = slice(128 * h, 128 * h + 128)
        here = fr[:, cols]
        above = jnp.where(row == 0, hv_rx[0, 7:8, cols] * has_up, pltpu.roll(here, 1, 0))
        below = jnp.where(row == TR - 1, hv_rx[1, 0:1, cols] * has_down, pltpu.roll(here, TR - 1, 0))
        there = fr[:, 128 - 128 * h : 256 - 128 * h]
        west_in = edges[0:TR] if h == 0 else pltpu.roll(there, 1, 1)
        east_in = pltpu.roll(there, 127, 1) if h == 0 else edges[TR : 2 * TR]
        west = jnp.where(lane == 0, west_in, pltpu.roll(here, 1, 1))
        east = jnp.where(lane == 127, east_in, pltpu.roll(here, 127, 1))
        total = e_ref[:, cols] + TAU * ((below + above) + (east + west))
        halves.append(total * (1.0 / TAU))
    U[1, 2 : GR - 2] = to_groups(lambda t, h: halves[h][8 * t : 8 * t + 8, :]).reshape(TR // 4, 8, 128)
    send_field(1)

    if mode == "fast":
        group_bytes(g1.at[0], 0, ND).wait_recv()
        m2[0] = jnp.sum(g1[0], axis=0)
        group_sends(m2.at[0], g2.at[0], 1, "col")

    def to_lines(f, dst, outside):
        @pl.when(home)
        def _():
            rx[f, j] = U[f, pl.ds(2 * m + 3 * core, 3)]

        one_less(home, rx.at[f], ND, rx_send.at[f], rx_recv.at[f], wait_recv)

        def ghosts(first, own_first, cond):
            @pl.when(cond)
            def _():
                self_too = ghost_from == i

                @pl.when(self_too)
                def _():
                    rxv[f, j] = U[f, pl.ds(own_first, 2)]

                one_less(self_too, rxv.at[f], ND, rxv_send.at[f], rxv_recv.at[f], wait_recv)
                for b in range(ND):
                    rx[f, b, first : first + 2] = rxv[f, b]

        ghosts(0, GR - 4, ghost_first)
        ghosts(1, 2, ghost_last)
        for g in range(3):
            at = pl.ds(384 * core + 128 * g, 128)
            S[f, at] = rx[f, :, g].reshape(128, 128).T
            pltpu.make_async_remote_copy(
                src_ref=S.at[f, at],
                dst_ref=S.at[f, at],
                send_sem=s_send.at[f],
                recv_sem=s_recv.at[f],
                device_id=(other, j),
                device_id_type=MESH,
            ).start()
        bytes_of(S.at[f, pl.ds(0, 384)], s_send.at[f], s_recv.at[f]).wait_recv()
        inside = MK[...] > 0.5
        for k in range(K):
            lines = jnp.concatenate(
                [S[f, pl.ds(256 * t + k, 8, stride=32), :] for t in range(3)], 0
            )
            dst[k] = jnp.where(inside, lines, outside)

    rows24 = iota((24, 128), 0)
    lanes24 = iota((24, 128), 1)
    lattice_row = 2 * TR * plane + 8 * (j - 1) + rows24
    MK[...] = jnp.where((lattice_row >= 0) & (lattice_row < TR * ND), 1.0, 0.0)

    to_lines(0, Y, 4.0)

    def after(x):
        return jnp.where(lanes24 == 127, 0.0, pltpu.roll(x, 127, 1))

    def before(x):
        return jnp.where(lanes24 == 0, 0.0, pltpu.roll(x, 1, 1))

    p = 1.0 / Y[0]
    inv[0] = p
    prod = p
    u[0] = prod
    for k in range(1, K - 1):
        p = 1.0 / (Y[k] - p)
        inv[k] = p
        prod = prod * p
        u[k] = prod
    last_u = prod
    q = p
    v[K - 2] = q
    w_u = prod
    for k in range(K - 3, -1, -1):
        p_k = inv[k]
        q = p_k * q
        v[k] = q
        w_u = u[k] + p_k * w_u
        u[k] = w_u
    pivot = 1.0 / (Y[K - 1] - p - after(w_u))
    lo_c = jnp.where(lanes24 == 0, 0.0, last_u) * pivot
    hi_c = after(last_u) * pivot
    levels = [{0: pivot}]
    for n in range(7):
        s = 1 << n
        d = 1.0 / (1.0 - lo_c * turn(hi_c, s) - hi_c * turn(lo_c, -s))
        a, b = d * lo_c, d * hi_c
        levels.append({0: d, s: a, 128 - s: b} if n < 6 else {0: d, s: a + b})
        lo_c = a * turn(lo_c, s)
        hi_c = b * turn(hi_c, -s)
    steps = (
        compose(levels[3], compose(levels[2], compose(levels[1], levels[0]))),
        compose(levels[7], compose(levels[6], compose(levels[5], levels[4]))),
    )
    offsets = [sorted(step) for step in steps]
    place = {}
    for n, step in enumerate(steps):
        for o in offsets[n]:
            place[n, o] = len(place)
            pcr[place[n, o]] = step[o]

    to_lines(1, RHS, 0.0)

    def solve(put):
        first = [u[k] * RHS[k] for k in range(4)]
        last = [v[k] * RHS[k] for k in range(4)]
        for k in range(4, K - 1):
            first[k % 4] = first[k % 4] + u[k] * RHS[k]
            last[k % 4] = last[k % 4] + v[k] * RHS[k]
        x = after((first[0] + first[1]) + (first[2] + first[3]))
        x = x + ((last[0] + last[1]) + (last[2] + last[3])) + RHS[K - 1]
        f = inv[0] * RHS[0]
        fs = [f]
        for k in range(1, K - 1):
            f = inv[k] * (RHS[k] + f)
            Y[k] = f
        for n in range(2):
            terms = [pcr[place[n, o]] * turn(x, o) for o in offsets[n]]
            while len(terms) > 1:
                terms = [sum(terms[t : t + 2][1:], terms[t]) for t in range(0, len(terms), 2)]
            x = terms[0]
        for k in range(K - 3, 0, -1):
            f = Y[k] + inv[k] * f
            Y[k] = f
        Y[0] = fs[0] + inv[0] * f
        prev = before(x)
        put(K - 1, x)
        for k in range(K - 2, -1, -1):
            put(k, Y[k] + (u[k] * prev + v[k] * x))

    def across(z):
        return MK[...] * (2.0 * z - (pltpu.roll(z, 1, 0) + pltpu.roll(z, 23, 0)))

    own = slice(8, 16)
    sub8 = iota((8, 128), 0)
    lane8 = iota((8, 128), 1)

    if mode == "fast":
        group_bytes(g2.at[0], 1, ND).wait_recv()
        mean = jnp.sum(jnp.sum(g2[0], axis=0), axis=(0, 1), keepdims=True) * (
            1.0 / float(TR * TC * ND * ND)
        )
        HV[...] = jnp.broadcast_to(0.5 * mean, (24, 128))
        zero = jnp.zeros((24, 128), f32)
        for n in (0, 1):
            for k in range(K):
                V[n, k] = zero
                RHO[n, k] = zero[own]

        def basis(it, _):
            w = jnp.where(it == 0, 1.0, HV[...])
            twice = jnp.where(it >= 2, 2.0, 1.0)

            def put(k, x):
                vec = twice * (x * w - V[it + 1, k]) - V[it, k]
                rho = twice * (RHS[k, own] * w[own] - RHO[it + 1, k]) - RHO[it, k]
                V[it + 2, k] = vec
                RHO[it + 2, k] = rho
                tv = across(vec)
                AV[it, k] = rho + tv[own]
                RHS[k] = tv

            solve(put)

            def dots(n, _):
                acc_a = [jnp.zeros((8, 128), f32)] * 4
                acc_n = [jnp.zeros((8, 128), f32)] * 4
                for k in range(K):
                    vec = V[it + 2, k, own]
                    acc_a[k % 4] = acc_a[k % 4] + vec * AV[n, k]
                    acc_n[k % 4] = acc_n[k % 4] + vec * RHO[n + 2, k]
                for first, acc in ((0, acc_a), (64, acc_n)):
                    total = jnp.sum((acc[0] + acc[1]) + (acc[2] + acc[3]), axis=0, keepdims=True)
                    GM[pl.ds(first + 56 - 8 * it + n, 1), :] = total
                    GM[pl.ds(first + 56 - 8 * n + it, 1), :] = total
                return 0

            lax.fori_loop(0, it + 1, dots, 0)
            return 0

        lax.fori_loop(0, ITERS, basis, 0)
        part = jnp.sum(GM[...].T, axis=0, keepdims=True)
        m1[1] = jnp.where(iota((W, 128), 0) == 0, part, 0.0)
        total = exchange(1)
        flat = jnp.sum(total, axis=0, keepdims=True)
        mat = pltpu.roll(jnp.broadcast_to(flat, (8, 128)), 0, 1, stride=8, stride_axis=0)
        worst = jnp.full((8, 1), 1.0, f32)
        diag0 = jnp.sum(jnp.where(lane8 == sub8 + 56, mat, 0.0), axis=1, keepdims=True)
        for n in range(ITERS):
            row_n = jnp.sum(jnp.where(sub8 == n, mat, 0.0), axis=0, keepdims=True)
            col_n = jnp.sum(jnp.where(lane8 == 56 + n, mat, 0.0), axis=1, keepdims=True)
            piv = jnp.sum(jnp.where(sub8[:, 0:1] == n, col_n, 0.0), axis=0, keepdims=True)
            first = jnp.sum(jnp.where(sub8[:, 0:1] == n, diag0, 0.0), axis=0, keepdims=True)
            worst = jnp.minimum(worst, jnp.broadcast_to(piv / first, (8, 1)))
            scaled = row_n / piv
            mat = jnp.where(sub8 == n, jnp.broadcast_to(scaled, (8, 128)), mat - col_n * scaled)
        coef = jnp.sum(jnp.where(lane8 == 120, mat, 0.0), axis=1, keepdims=True)
        coef = jnp.broadcast_to(coef, (8, 128))
        odd = core
        coef = coef * jnp.where(odd == 1, -TAU, 1.0)
        base = jnp.where(odd == 1, TAU, 0.0)
        flag_out[0] = jnp.where(jnp.min(worst) > PIVOT_MIN, 1, 0)
        weights = [jnp.broadcast_to(coef[n : n + 1, :], (8, 128)) for n in range(ITERS)]

        @pl.when(odd == 0)
        def _():
            for k in range(K):
                acc = weights[0] * V[2, k, own]
                for n in range(1, ITERS):
                    acc = acc + weights[n] * V[n + 2, k, own]
                S2[pl.ds(k, 8, stride=32), :] = acc

        @pl.when(odd == 1)
        def _():
            for k in range(K):
                acc = weights[0] * AV[0, k]
                for n in range(1, ITERS):
                    acc = acc + weights[n] * AV[n, k]
                S2[pl.ds(k, 8, stride=32), :] = acc + base * RHO[2, k]

    else:
        zero = jnp.zeros((24, 128), f32)
        for n in (3, 4, 5):
            for k in range(K):
                V[n, k] = zero

        def iterate(it, carry):
            gamma_old, alpha_old = carry
            acc = [jnp.zeros((8, 128), f32)] * 4

            def put(k, x):
                r = RHS[k]
                w = MK[...] * r + across(x)
                V[2, k] = x
                V[6, k] = w
                acc[k % 2] = acc[k % 2] + x[own] * r[own]
                acc[2 + k % 2] = acc[2 + k % 2] + x[own] * w[own]

            solve(put)
            gam = jnp.sum(acc[0] + acc[1], axis=0, keepdims=True)
            mu = jnp.sum(acc[2] + acc[3], axis=0, keepdims=True)
            m1[it] = jnp.where(iota((W, 128), 0) == 0, gam, mu)
            total = jnp.sum(exchange(it), axis=1, keepdims=True)
            gamma = total[0:1]
            mu = total[1:2]
            beta = jnp.where(it == 0, 0.0, gamma / gamma_old)
            alpha = gamma / (mu - beta * gamma / alpha_old)
            for k in range(K):
                p = V[2, k] + beta * V[3, k]
                s = V[6, k] + beta * V[4, k]
                V[3, k] = p
                V[4, k] = s
                V[5, k] = V[5, k] + alpha * p
                RHS[k] = RHS[k] - alpha * s
            return gamma, alpha

        one = jnp.ones((1, 1), f32)
        lax.fori_loop(0, ITERS, iterate, (one, one))
        odd = core
        flag_out[0] = 1

        @pl.when(odd == 0)
        def _():
            for k in range(K):
                S2[pl.ds(k, 8, stride=32), :] = V[5, k, own]

        @pl.when(odd == 1)
        def _():
            for k in range(K):
                S2[pl.ds(k, 8, stride=32), :] = TAU * RHS[k, own]

    for g in range(2):
        OM[:, g] = S2[128 * g : 128 * g + 128].T.reshape(ND, 8, 128)
    slot = 2 * m + core
    for d in range(ND):
        b = (j + d) % ND

        def start():
            pltpu.make_async_remote_copy(
                src_ref=OM.at[b],
                dst_ref=ORX.at[slot],
                send_sem=o_send,
                recv_sem=o_recv,
                device_id=(block, b),
                device_id_type=MESH,
            ).start()

        if d == 0:
            pl.when(jnp.logical_not(home))(start)
        else:
            start()

    @pl.when(home)
    def _():
        ORX[slot] = OM[j]

    one_less(home, ORX, ND, o_send, o_recv, wait_recv)
    low = iota((8, 128), 0) < 4
    for which, out in ((0, x_out), (1, r_out)):
        groups = jnp.concatenate([ORX[2 * t + which, g] for t in range(TR // 8) for g in range(2)], 0)
        groups = seg_transpose(groups)
        for t in range(TR // 8):
            a = groups[16 * t : 16 * t + 8]
            b = groups[16 * t + 8 : 16 * t + 16]
            out[8 * t : 8 * t + 8, 0:128] = jnp.where(low, a, pltpu.roll(b, 4, 0))
            out[8 * t : 8 * t + 8, 128:256] = jnp.where(low, pltpu.roll(a, 4, 0), b)

    one_less(home, ORX, ND, o_send, o_recv, wait_send)
    for c in halos:
        c.wait_send()
    for f in (0, 1):
        one_less(home, rx.at[f], ND, rx_send.at[f], rx_recv.at[f], wait_send)
        bytes_of(S.at[f, pl.ds(0, 384)], s_send.at[f], s_recv.at[f]).wait_send()
        one_less(
            below_self | above_self, rxv.at[f], 2, rxv_send.at[f], rxv_recv.at[f], wait_send
        )
    for slot in range(2 if mode == "fast" else ITERS):
        first = slot == 0 and mode == "fast"
        group_bytes(g1.at[slot], 2 * slot, ND).wait_send()
        group_bytes(g2.at[slot], 2 * slot + 1, ND if first else ND // 2).wait_send()


def run(mode, events, entry_week, exit_week, log_offset, frailty, kappa_sq, log_rate, shape_rate):
    slots = 2 if mode == "fast" else ITERS
    vm = pltpu.VMEM
    dma = pltpu.SemaphoreType.DMA
    return pl.pallas_call(
        functools.partial(kernel, mode),
        out_shape=(
            jax.ShapeDtypeStruct((TR, TC), f32),
            jax.ShapeDtypeStruct((TR, TC), f32),
            jax.ShapeDtypeStruct((1,), jnp.int32),
        ),
        in_specs=[pl.BlockSpec(memory_space=pltpu.HBM)] * 8,
        out_specs=(
            pl.BlockSpec(memory_space=pltpu.VMEM),
            pl.BlockSpec(memory_space=pltpu.VMEM),
            pl.BlockSpec(memory_space=pltpu.SMEM),
        ),
        scratch_shapes=[
            pltpu.SMEM((1,), f32),
            pltpu.SMEM((1,), f32),
            vm(events.shape, jnp.int32),
            vm((TR, TC), jnp.int32),
            vm((TR, TC), jnp.int32),
            vm((TR, TC), f32),
            vm((TR, TC), f32),
            vm((TR, TC), f32),
            vm((TR, TC), f32),
            vm((2, 8, TC), f32),
            vm((2, 8, 128), f32),
            vm((2, 8, 128), f32),
            vm((2, GR, 8, 128), f32),
            vm((2, ND, 3, 8, 128), f32),
            vm((2, ND, 2, 8, 128), f32),
            vm((2, 768, 128), f32),
            vm((K, 24, 128), f32),
            vm((K, 24, 128), f32),
            vm((K, 24, 128), f32),
            vm((31, 24, 128), f32),
            vm((K, 24, 128), f32),
            vm((K, 24, 128), f32),
            vm((ITERS + 2, K, 24, 128), f32),
            vm((ITERS + 2, K, 8, 128), f32),
            vm((ITERS, K, 8, 128), f32),
            vm((24, 128), f32),
            vm((24, 128), f32),
            vm((128, 128), f32),
            vm((slots, W, 128), f32),
            vm((slots, W, 128), f32),
            vm((slots, ND, W, 128), f32),
            vm((slots, ND, W, 128), f32),
            vm((256, 128), f32),
            vm((ND, 2, 8, 128), f32),
            vm((ND, 2, 8, 128), f32),
            dma((7 + EV_PARTS,)),
            dma((4,)),
            dma((4,)),
            dma((2,)),
            dma((2,)),
            dma((2,)),
            dma((2,)),
            dma((2 * slots,)),
            dma((2 * slots,)),
            dma,
            dma,
            dma((2,)),
            dma((2,)),
        ],
        compiler_params=pltpu.CompilerParams(
            collective_id=0 if mode == "fast" else 1,
            has_side_effects=True,
            vmem_limit_bytes=40 * 2**20,
        ),
        name="newton_" + mode,
    )(log_rate, shape_rate, events, entry_week, exit_week, log_offset, frailty, kappa_sq)


def per_device(*args):
    step, residual, flag = run("fast", *args)
    return lax.cond(
        flag[0] > 0,
        lambda: (step, residual),
        lambda: tuple(run("cg", *args)[:2]),
    )


def solution(mesh):
    tile = P("row", "col")
    return jax.shard_map(
        per_device,
        mesh=mesh,
        in_specs=(P(None, "row", "col"), tile, tile, tile, tile, tile, P(), P()),
        out_specs=(tile, tile),
        check_vma=False,
    )
```

```python
import functools

import jax
import jax.numpy as jnp
from jax import lax
from jax.experimental import pallas as pl
from jax.experimental.pallas import tpu as pltpu
from jax.sharding import PartitionSpec as P


ITERS = 8
TAU = 16.0
MESH = pl.DeviceIdType.MESH
TR, TC = 64, 256
ND = 16
K = 32
GR = 20
EV_PARTS = 4
PIVOT_MIN = 2e-3
W = 2
f32 = jnp.float32


def iota(shape, dim):
    return lax.broadcasted_iota(jnp.int32, shape, dim)


def turn(x, by):
    by = by % 128
    return pltpu.roll(x, by, 1) if by else x


def compose(later, earlier):
    out = {}
    for o, x in later.items():
        for q, y in earlier.items():
            term = x * turn(y, o)
            at = (o + q) % 128
            out[at] = out[at] + term if at in out else term
    return out


def seg_transpose(x):
    sub = iota(x.shape, 0) % 4
    seg = iota(x.shape, 1) // 32
    n = x.shape[0]
    out = x
    for d in (1, 2, 3):
        y = jnp.where(sub + d < 4, pltpu.roll(x, n - d, 0), pltpu.roll(x, 4 - d, 0))
        y = pltpu.roll(y, 32 * d, 1)
        out = jnp.where((seg - sub + 4) % 4 == d, y, out)
    return out


def to_groups(tile_of):
    low = iota((8, 128), 0) < 4
    parts = []
    for t in range(TR // 8):
        a, b = tile_of(t, 0), tile_of(t, 1)
        parts.append(jnp.where(low, a, pltpu.roll(b, 4, 0)))
        parts.append(jnp.where(low, pltpu.roll(a, 4, 0), b))
    return seg_transpose(jnp.concatenate(parts, 0))


def kernel(
    mode,
    lr_hbm,
    sr_hbm,
    ev_hbm,
    en_hbm,
    ex_hbm,
    lo_hbm,
    fr_hbm,
    ka_hbm,
    both_out,
    flag_out,
    lr_ref,
    sr_ref,
    ev,
    en,
    ex,
    lo,
    fr,
    ka,
    e_ref,
    hv_rx,
    hh_tx,
    hh_rx,
    U,
    rx,
    rxv,
    S,
    inv,
    u,
    v,
    pcr,
    Y,
    RHS,
    V,
    RHO,
    AV,
    MK,
    HV,
    GM,
    m1,
    m2,
    g1,
    g2,
    S2,
    OM,
    ORX,
    in_sem,
    hal_send,
    hal_recv,
    rx_send,
    rx_recv,
    rxv_send,
    rxv_recv,
    g_send,
    g_recv,
    o_send,
    o_recv,
    s_send,
    s_recv,
):
    i = lax.axis_index("row")
    j = lax.axis_index("col")
    plane, core = i // 2, i % 2
    m = j % 8
    block = 2 * plane + j // 8
    other = i + 1 - 2 * core
    home = block == i
    up_i, down_i = (i + ND - 1) % ND, (i + 1) % ND
    left_j, right_j = (j + ND - 1) % ND, (j + 1) % ND

    barrier = pltpu.get_barrier_semaphore()

    def hello(a, b):
        pl.semaphore_signal(barrier, inc=1, device_id=(a, b), device_id_type=MESH)

    for d in range(1, ND):
        hello(i, (j + d) % ND)
    for d in range(1, ND):
        hello((i + d) % ND, j)
    for d in range(8):
        hello(other, 8 * core + d)

    @pl.when(jnp.logical_not(home))
    def _():
        for b in range(ND):
            hello(other, b)

    ghost_first = (core == 0) & (m == 0)
    ghost_last = (core == 1) & (m == 7)
    ghost_from = (block + jnp.where(core == 0, ND - 1, 1)) % ND
    below_dev = (2 * (down_i // 2), 8 * (down_i % 2))
    above_dev = (2 * (up_i // 2) + 1, 8 * (up_i % 2) + 7)
    below_self = (below_dev[0] == i) & (below_dev[1] == j)
    above_self = (above_dev[0] == i) & (above_dev[1] == j)

    @pl.when(ghost_first | ghost_last)
    def _():
        for b in range(ND):

            @pl.when(jnp.logical_not((ghost_from == i) & (j == b)))
            def _():
                hello(ghost_from, b)

    loads = [
        pltpu.make_async_copy(src, dst, in_sem.at[n])
        for n, (src, dst) in enumerate(
            (
                (fr_hbm, fr),
                (ex_hbm, ex),
                (en_hbm, en),
                (lo_hbm, lo),
                (ka_hbm, ka),
                (lr_hbm, lr_ref),
                (sr_hbm, sr_ref),
            )
        )
    ]
    weeks = ev.shape[0] // EV_PARTS
    ev_loads = [
        pltpu.make_async_copy(
            ev_hbm.at[pl.ds(n * weeks, weeks)], ev.at[pl.ds(n * weeks, weeks)], in_sem.at[7 + n]
        )
        for n in range(EV_PARTS)
    ]
    for c in loads + ev_loads:
        c.start()
    for c in loads:
        c.wait()

    flipped = jnp.concatenate([fr[:, 128:256], fr[:, 0:128]], 0).T
    hh_tx[0] = flipped[120:128]
    hh_tx[1] = flipped[0:8]
    rate = jnp.full((1, TC), sr_ref[0], f32)
    scale = jnp.exp(jnp.full((1, TC), lr_ref[0], f32)) / rate
    slope = rate / float(ev.shape[0])
    exposure = scale * (jnp.exp(slope * ex[...].astype(f32)) - jnp.exp(slope * en[...].astype(f32)))
    weight = exposure * jnp.exp(lo[...] + fr[...])
    e_ref[...] = -weight - TAU * (4.0 + ka[...]) * fr[...]
    diag = 2.0 + ka[...] + weight * (1.0 / TAU)

    fill = iota((2, 8, 128), 0) * 0
    for f, value in ((0, 4.0), (1, 0.0)):
        U[f, 0:2] = fill.astype(f32) + value
        U[f, GR - 2 : GR] = fill.astype(f32) + value
    U[0, 2 : GR - 2] = to_groups(
        lambda t, h: diag[8 * t : 8 * t + 8, 128 * h : 128 * h + 128]
    ).reshape(TR // 4, 8, 128)
    part = diag - 2.0
    part = part[:, 0:128] + part[:, 128:256]
    part = jnp.sum(part, axis=0, keepdims=True)
    m1[0] = jnp.where(iota((W, 128), 0) == 0, part, 0.0)

    def send_field(f):
        for q in (0, 1):
            for d in range(8):
                a = (m + d) % 8
                to = core if q == 0 else 1 - core
                src = U.at[f, pl.ds(2 * a + 3 * to, 3)]

                def start():
                    pltpu.make_async_remote_copy(
                        src_ref=src,
                        dst_ref=rx.at[f, j],
                        send_sem=rx_send.at[f],
                        recv_sem=rx_recv.at[f],
                        device_id=(2 * plane + to, 8 * core + a),
                        device_id_type=MESH,
                    ).start()

                if q == 0 and d == 0:
                    pl.when(jnp.logical_not(home))(start)
                else:
                    start()
        for first, to, here in ((GR - 4, below_dev, below_self), (2, above_dev, above_self)):
            src = U.at[f, pl.ds(first, 2)]

            @pl.when(jnp.logical_not(here))
            def _():
                pltpu.make_async_remote_copy(
                    src_ref=src,
                    dst_ref=rxv.at[f, j],
                    send_sem=rxv_send.at[f],
                    recv_sem=rxv_recv.at[f],
                    device_id=to,
                    device_id_type=MESH,
                ).start()

    def bytes_of(ref, send, recv):
        return pltpu.make_async_remote_copy(
            src_ref=ref,
            dst_ref=ref,
            send_sem=send,
            recv_sem=recv,
            device_id=(i, right_j),
            device_id_type=MESH,
        )

    def one_less(cond, ref, count, send, recv, act):
        @pl.when(cond)
        def _():
            act(bytes_of(ref.at[pl.ds(0, count - 1)], send, recv))

        @pl.when(jnp.logical_not(cond))
        def _():
            act(bytes_of(ref.at[pl.ds(0, count)], send, recv))

    def wait_recv(c):
        c.wait_recv()

    def wait_send(c):
        c.wait_send()

    def group_sends(src, dst, sem, axis):
        if axis == "col":
            me, to = j, [(i, (j + d) % ND) for d in range(1, ND)]
        elif axis == "row":
            me, to = i, [((i + d) % ND, j) for d in range(1, ND)]
        else:
            me, to = plane, [((i + 2 * d) % ND, j) for d in range(1, ND // 2)]
        for dev in to:
            pltpu.make_async_remote_copy(
                src_ref=src,
                dst_ref=dst.at[me],
                send_sem=g_send.at[sem],
                recv_sem=g_recv.at[sem],
                device_id=dev,
                device_id_type=MESH,
            ).start()
        dst[me] = src[...]

    def group_bytes(dst, sem, count):
        return bytes_of(dst.at[pl.ds(0, count - 1)], g_send.at[sem], g_recv.at[sem])

    def exchange(slot):
        group_sends(m1.at[slot], g1.at[slot], 2 * slot, "col")
        group_bytes(g1.at[slot], 2 * slot, ND).wait_recv()
        m2[slot] = jnp.sum(g1[slot], axis=0)
        group_sends(m2.at[slot], g2.at[slot], 2 * slot + 1, "plane")
        group_bytes(g2.at[slot], 2 * slot + 1, ND // 2).wait_recv()
        return jnp.sum(g2[slot, 0 : ND // 2], axis=0)

    greeted = 2 * (ND - 1) + 8 + 2
    greeted = greeted + jnp.where(home, 0, ND)
    greeted = greeted - jnp.where(below_self, 1, 0) - jnp.where(above_self, 1, 0)
    pl.semaphore_wait(barrier, greeted)

    halos = [
        pltpu.make_async_remote_copy(
            src_ref=src,
            dst_ref=dst,
            send_sem=hal_send.at[n],
            recv_sem=hal_recv.at[n],
            device_id=dev,
            device_id_type=MESH,
        )
        for n, (src, dst, dev) in enumerate(
            (
                (fr.at[pl.ds(TR - 8, 8)], hv_rx.at[0], (down_i, j)),
                (fr.at[pl.ds(0, 8)], hv_rx.at[1], (up_i, j)),
                (hh_tx.at[0], hh_rx.at[0], (i, right_j)),
                (hh_tx.at[1], hh_rx.at[1], (i, left_j)),
            )
        )
    ]
    for c in halos:
        c.start()
    send_field(0)
    if mode == "fast":
        group_sends(m1.at[0], g1.at[0], 0, "row")

    en_v, ex_v = en[...], ex[...]
    count = jnp.zeros((TR, TC), jnp.int32)
    for n in range(EV_PARTS):
        ev_loads[n].wait()

        def add_week(w, acc):
            week = w + n * weeks
            at_risk = (week >= en_v) & (week < ex_v)
            return acc + jnp.where(at_risk, ev[week], 0)

        count = lax.fori_loop(0, weeks, add_week, count)
    e_ref[...] = e_ref[...] + count.astype(f32)

    for c in halos:
        c.wait_recv()
    row = iota((TR, 128), 0)
    lane = iota((TR, 128), 1)
    has_up, has_down = jnp.where(i > 0, 1.0, 0.0), jnp.where(i < ND - 1, 1.0, 0.0)
    has_left, has_right = jnp.where(j > 0, 1.0, 0.0), jnp.where(j < ND - 1, 1.0, 0.0)
    lane1 = iota((1, 128), 1)
    edges = jnp.where(lane1 < TR, hh_rx[0, 7:8] * has_left, hh_rx[1, 0:1] * has_right)
    edges = jnp.broadcast_to(edges, (128, 128)).T
    halves = []
    for h in (0, 1):
        cols = slice(128 * h, 128 * h + 128)
        here = fr[:, cols]
        above = jnp.where(row == 0, hv_rx[0, 7:8, cols] * has_up, pltpu.roll(here, 1, 0))
        below = jnp.where(row == TR - 1, hv_rx[1, 0:1, cols] * has_down, pltpu.roll(here, TR - 1, 0))
        there = fr[:, 128 - 128 * h : 256 - 128 * h]
        west_in = edges[0:TR] if h == 0 else pltpu.roll(there, 1, 1)
        east_in = pltpu.roll(there, 127, 1) if h == 0 else edges[TR : 2 * TR]
        west = jnp.where(lane == 0, west_in, pltpu.roll(here, 1, 1))
        east = jnp.where(lane == 127, east_in, pltpu.roll(here, 127, 1))
        total = e_ref[:, cols] + TAU * ((below + above) + (east + west))
        halves.append(total * (1.0 / TAU))
    U[1, 2 : GR - 2] = to_groups(lambda t, h: halves[h][8 * t : 8 * t + 8, :]).reshape(TR // 4, 8, 128)
    send_field(1)

    if mode == "fast":
        group_bytes(g1.at[0], 0, ND).wait_recv()
        m2[0] = jnp.sum(g1[0], axis=0)
        group_sends(m2.at[0], g2.at[0], 1, "col")

    def to_lines(f, dst, outside):
        @pl.when(home)
        def _():
            rx[f, j] = U[f, pl.ds(2 * m + 3 * core, 3)]

        one_less(home, rx.at[f], ND, rx_send.at[f], rx_recv.at[f], wait_recv)

        def ghosts(first, own_first, cond):
            @pl.when(cond)
            def _():
                self_too = ghost_from == i

                @pl.when(self_too)
                def _():
                    rxv[f, j] = U[f, pl.ds(own_first, 2)]

                one_less(self_too, rxv.at[f], ND, rxv_send.at[f], rxv_recv.at[f], wait_recv)
                for b in range(ND):
                    rx[f, b, first : first + 2] = rxv[f, b]

        ghosts(0, GR - 4, ghost_first)
        ghosts(1, 2, ghost_last)
        for g in range(3):
            at = pl.ds(384 * core + 128 * g, 128)
            S[f, at] = rx[f, :, g].reshape(128, 128).T
            pltpu.make_async_remote_copy(
                src_ref=S.at[f, at],
                dst_ref=S.at[f, at],
                send_sem=s_send.at[f],
                recv_sem=s_recv.at[f],
                device_id=(other, j),
                device_id_type=MESH,
            ).start()
        bytes_of(S.at[f, pl.ds(0, 384)], s_send.at[f], s_recv.at[f]).wait_recv()
        inside = MK[...] > 0.5
        for k in range(K):
            lines = jnp.concatenate(
                [S[f, pl.ds(256 * t + k, 8, stride=32), :] for t in range(3)], 0
            )
            dst[k] = jnp.where(inside, lines, outside)

    rows24 = iota((24, 128), 0)
    lanes24 = iota((24, 128), 1)
    lattice_row = 2 * TR * plane + 8 * (j - 1) + rows24
    MK[...] = jnp.where((lattice_row >= 0) & (lattice_row < TR * ND), 1.0, 0.0)

    to_lines(0, Y, 4.0)

    def after(x):
        return jnp.where(lanes24 == 127, 0.0, pltpu.roll(x, 127, 1))

    def before(x):
        return jnp.where(lanes24 == 0, 0.0, pltpu.roll(x, 1, 1))

    p = MK[...] / Y[0]
    inv[0] = p
    prod = p
    u[0] = prod
    for k in range(1, K - 1):
        p = MK[...] / (Y[k] - p)
        inv[k] = p
        prod = prod * p
        u[k] = prod
    last_u = prod
    q = p
    v[K - 2] = q
    w_u = prod
    for k in range(K - 3, -1, -1):
        p_k = inv[k]
        q = p_k * q
        v[k] = q
        w_u = u[k] + p_k * w_u
        u[k] = w_u
    pivot = MK[...] / (Y[K - 1] - p - after(w_u))
    lo_c = jnp.where(lanes24 == 0, 0.0, last_u) * pivot
    hi_c = after(last_u) * pivot
    levels = [{0: pivot}]
    for n in range(7):
        s = 1 << n
        d = 1.0 / (1.0 - lo_c * turn(hi_c, s) - hi_c * turn(lo_c, -s))
        a, b = d * lo_c, d * hi_c
        levels.append({0: d, s: a, 128 - s: b} if n < 6 else {0: d, s: a + b})
        lo_c = a * turn(lo_c, s)
        hi_c = b * turn(hi_c, -s)
    steps = (
        compose(levels[3], compose(levels[2], compose(levels[1], levels[0]))),
        compose(levels[7], compose(levels[6], compose(levels[5], levels[4]))),
    )
    offsets = [sorted(step) for step in steps]
    place = {}
    for n, step in enumerate(steps):
        for o in offsets[n]:
            place[n, o] = len(place)
            pcr[place[n, o]] = step[o]

    to_lines(1, RHS, 0.0)

    def solve(put):
        first = [u[k] * RHS[k] for k in range(4)]
        last = [v[k] * RHS[k] for k in range(4)]
        for k in range(4, K - 1):
            first[k % 4] = first[k % 4] + u[k] * RHS[k]
            last[k % 4] = last[k % 4] + v[k] * RHS[k]
        x = after((first[0] + first[1]) + (first[2] + first[3]))
        x = x + ((last[0] + last[1]) + (last[2] + last[3])) + RHS[K - 1]
        f = inv[0] * RHS[0]
        fs = [f]
        for k in range(1, K - 1):
            f = inv[k] * (RHS[k] + f)
            Y[k] = f
        for n in range(2):
            terms = [pcr[place[n, o]] * turn(x, o) for o in offsets[n]]
            while len(terms) > 1:
                terms = [sum(terms[t : t + 2][1:], terms[t]) for t in range(0, len(terms), 2)]
            x = terms[0]
        for k in range(K - 3, 0, -1):
            f = Y[k] + inv[k] * f
            Y[k] = f
        Y[0] = fs[0] + inv[0] * f
        prev = before(x)
        put(K - 1, x)
        for k in range(K - 2, -1, -1):
            put(k, Y[k] + (u[k] * prev + v[k] * x))

    def across(z):
        return 2.0 * z - (pltpu.roll(z, 1, 0) + pltpu.roll(z, 23, 0))

    own = slice(8, 16)
    sub8 = iota((8, 128), 0)
    lane8 = iota((8, 128), 1)

    if mode == "fast":
        group_bytes(g2.at[0], 1, ND).wait_recv()
        mean = jnp.sum(jnp.sum(g2[0], axis=0), axis=(0, 1), keepdims=True) * (
            1.0 / float(TR * TC * ND * ND)
        )
        HV[...] = jnp.broadcast_to(0.5 * mean, (24, 128))
        zero = jnp.zeros((24, 128), f32)
        for n in (0, 1):
            for k in range(K):
                V[n, k] = zero
                RHO[n, k] = zero[own]

        def basis(it, _):
            w = jnp.where(it == 0, 1.0, HV[...])
            twice = jnp.where(it >= 2, 2.0, 1.0)

            def put(k, x):
                vec = twice * (x * w - V[it + 1, k]) - V[it, k]
                rho = twice * (RHS[k, own] * w[own] - RHO[it + 1, k]) - RHO[it, k]
                V[it + 2, k] = vec
                RHO[it + 2, k] = rho
                tv = across(vec)
                AV[it, k] = rho + tv[own]
                RHS[k] = tv

            solve(put)

            def dots(n, _):
                acc_a = [jnp.zeros((8, 128), f32)] * 4
                acc_n = [jnp.zeros((8, 128), f32)] * 4
                for k in range(K):
                    vec = V[it + 2, k, own]
                    acc_a[k % 4] = acc_a[k % 4] + vec * AV[n, k]
                    acc_n[k % 4] = acc_n[k % 4] + vec * RHO[n + 2, k]
                for first, acc in ((0, acc_a), (64, acc_n)):
                    total = jnp.sum((acc[0] + acc[1]) + (acc[2] + acc[3]), axis=0, keepdims=True)
                    GM[pl.ds(first + 56 - 8 * it + n, 1), :] = total
                    GM[pl.ds(first + 56 - 8 * n + it, 1), :] = total
                return 0

            lax.fori_loop(0, it + 1, dots, 0)
            return 0

        lax.fori_loop(0, ITERS, basis, 0)
        part = jnp.sum(GM[...].T, axis=0, keepdims=True)
        m1[1] = jnp.where(iota((W, 128), 0) == 0, part, 0.0)
        total = exchange(1)
        flat = jnp.sum(total, axis=0, keepdims=True)
        mat = pltpu.roll(jnp.broadcast_to(flat, (8, 128)), 0, 1, stride=8, stride_axis=0)
        worst = jnp.full((8, 1), 1.0, f32)
        diag0 = jnp.sum(jnp.where(lane8 == sub8 + 56, mat, 0.0), axis=1, keepdims=True)
        for n in range(ITERS):
            row_n = jnp.sum(jnp.where(sub8 == n, mat, 0.0), axis=0, keepdims=True)
            col_n = jnp.sum(jnp.where(lane8 == 56 + n, mat, 0.0), axis=1, keepdims=True)
            piv = jnp.sum(jnp.where(sub8[:, 0:1] == n, col_n, 0.0), axis=0, keepdims=True)
            first = jnp.sum(jnp.where(sub8[:, 0:1] == n, diag0, 0.0), axis=0, keepdims=True)
            worst = jnp.minimum(worst, jnp.broadcast_to(piv / first, (8, 1)))
            scaled = row_n / piv
            mat = jnp.where(sub8 == n, jnp.broadcast_to(scaled, (8, 128)), mat - col_n * scaled)
        coef = jnp.sum(jnp.where(lane8 == 120, mat, 0.0), axis=1, keepdims=True)
        coef = jnp.broadcast_to(coef, (8, 128))
        odd = core
        coef = coef * jnp.where(odd == 1, -TAU, 1.0)
        base = jnp.where(odd == 1, TAU, 0.0)
        flag_out[0] = jnp.where(jnp.min(worst) > PIVOT_MIN, 1, 0)
        weights = [jnp.broadcast_to(coef[n : n + 1, :], (8, 128)) for n in range(ITERS)]

        @pl.when(odd == 0)
        def _():
            for k in range(K):
                acc = weights[0] * V[2, k, own]
                for n in range(1, ITERS):
                    acc = acc + weights[n] * V[n + 2, k, own]
                S2[pl.ds(k, 8, stride=32), :] = acc

        @pl.when(odd == 1)
        def _():
            for k in range(K):
                acc = weights[0] * AV[0, k]
                for n in range(1, ITERS):
                    acc = acc + weights[n] * AV[n, k]
                S2[pl.ds(k, 8, stride=32), :] = acc + base * RHO[2, k]

    else:
        zero = jnp.zeros((24, 128), f32)
        for n in (3, 4, 5):
            for k in range(K):
                V[n, k] = zero

        def iterate(it, carry):
            gamma_old, alpha_old = carry
            acc = [jnp.zeros((8, 128), f32)] * 4

            def put(k, x):
                r = RHS[k]
                w = MK[...] * r + across(x)
                V[2, k] = x
                V[6, k] = w
                acc[k % 2] = acc[k % 2] + x[own] * r[own]
                acc[2 + k % 2] = acc[2 + k % 2] + x[own] * w[own]

            solve(put)
            gam = jnp.sum(acc[0] + acc[1], axis=0, keepdims=True)
            mu = jnp.sum(acc[2] + acc[3], axis=0, keepdims=True)
            m1[it] = jnp.where(iota((W, 128), 0) == 0, gam, mu)
            total = jnp.sum(exchange(it), axis=1, keepdims=True)
            gamma = total[0:1]
            mu = total[1:2]
            beta = jnp.where(it == 0, 0.0, gamma / gamma_old)
            alpha = gamma / (mu - beta * gamma / alpha_old)
            for k in range(K):
                p = V[2, k] + beta * V[3, k]
                s = V[6, k] + beta * V[4, k]
                V[3, k] = p
                V[4, k] = s
                V[5, k] = V[5, k] + alpha * p
                RHS[k] = RHS[k] - alpha * s
            return gamma, alpha

        one = jnp.ones((1, 1), f32)
        lax.fori_loop(0, ITERS, iterate, (one, one))
        odd = core
        flag_out[0] = 1

        @pl.when(odd == 0)
        def _():
            for k in range(K):
                S2[pl.ds(k, 8, stride=32), :] = V[5, k, own]

        @pl.when(odd == 1)
        def _():
            for k in range(K):
                S2[pl.ds(k, 8, stride=32), :] = TAU * RHS[k, own]

    for g in range(2):
        OM[:, g] = S2[128 * g : 128 * g + 128].T.reshape(ND, 8, 128)
    slot = 2 * m + core
    for d in range(ND):
        b = (j + d) % ND

        def start():
            pltpu.make_async_remote_copy(
                src_ref=OM.at[b],
                dst_ref=ORX.at[slot],
                send_sem=o_send,
                recv_sem=o_recv,
                device_id=(block, b),
                device_id_type=MESH,
            ).start()

        if d == 0:
            pl.when(jnp.logical_not(home))(start)
        else:
            start()

    @pl.when(home)
    def _():
        ORX[slot] = OM[j]

    one_less(home, ORX, ND, o_send, o_recv, wait_recv)
    low = iota((8, 128), 0) < 4
    for which in (0, 1):
        groups = jnp.concatenate([ORX[2 * t + which, g] for t in range(TR // 8) for g in range(2)], 0)
        groups = seg_transpose(groups)
        for t in range(TR // 8):
            a = groups[16 * t : 16 * t + 8]
            b = groups[16 * t + 8 : 16 * t + 16]
            both_out[which, 8 * t : 8 * t + 8, 0:128] = jnp.where(low, a, pltpu.roll(b, 4, 0))
            both_out[which, 8 * t : 8 * t + 8, 128:256] = jnp.where(low, pltpu.roll(a, 4, 0), b)

    one_less(home, ORX, ND, o_send, o_recv, wait_send)
    for c in halos:
        c.wait_send()
    for f in (0, 1):
        one_less(home, rx.at[f], ND, rx_send.at[f], rx_recv.at[f], wait_send)
        bytes_of(S.at[f, pl.ds(0, 384)], s_send.at[f], s_recv.at[f]).wait_send()
        one_less(
            below_self | above_self, rxv.at[f], 2, rxv_send.at[f], rxv_recv.at[f], wait_send
        )
    for slot in range(2 if mode == "fast" else ITERS):
        first = slot == 0 and mode == "fast"
        group_bytes(g1.at[slot], 2 * slot, ND).wait_send()
        group_bytes(g2.at[slot], 2 * slot + 1, ND if first else ND // 2).wait_send()


def run(mode, events, entry_week, exit_week, log_offset, frailty, kappa_sq, log_rate, shape_rate):
    slots = 2 if mode == "fast" else ITERS
    vm = pltpu.VMEM
    dma = pltpu.SemaphoreType.DMA
    return pl.pallas_call(
        functools.partial(kernel, mode),
        out_shape=(
            jax.ShapeDtypeStruct((2, TR, TC), f32),
            jax.ShapeDtypeStruct((1,), jnp.int32),
        ),
        in_specs=[pl.BlockSpec(memory_space=pltpu.HBM)] * 8,
        out_specs=(
            pl.BlockSpec(memory_space=pltpu.VMEM),
            pl.BlockSpec(memory_space=pltpu.SMEM),
        ),
        scratch_shapes=[
            pltpu.SMEM((1,), f32),
            pltpu.SMEM((1,), f32),
            vm(events.shape, jnp.int32),
            vm((TR, TC), jnp.int32),
            vm((TR, TC), jnp.int32),
            vm((TR, TC), f32),
            vm((TR, TC), f32),
            vm((TR, TC), f32),
            vm((TR, TC), f32),
            vm((2, 8, TC), f32),
            vm((2, 8, 128), f32),
            vm((2, 8, 128), f32),
            vm((2, GR, 8, 128), f32),
            vm((2, ND, 3, 8, 128), f32),
            vm((2, ND, 2, 8, 128), f32),
            vm((2, 800, 128), f32),
            vm((K, 24, 128), f32),
            vm((K, 24, 128), f32),
            vm((K, 24, 128), f32),
            vm((31, 24, 128), f32),
            vm((K, 24, 128), f32),
            vm((K, 24, 128), f32),
            vm((ITERS + 2, K, 24, 128), f32),
            vm((ITERS + 2, K, 8, 128), f32),
            vm((ITERS, K, 8, 128), f32),
            vm((24, 128), f32),
            vm((24, 128), f32),
            vm((128, 128), f32),
            vm((slots, W, 128), f32),
            vm((slots, W, 128), f32),
            vm((slots, ND, W, 128), f32),
            vm((slots, ND, W, 128), f32),
            vm((288, 128), f32),
            vm((ND, 2, 8, 128), f32),
            vm((ND, 2, 8, 128), f32),
            dma((7 + EV_PARTS,)),
            dma((4,)),
            dma((4,)),
            dma((2,)),
            dma((2,)),
            dma((2,)),
            dma((2,)),
            dma((2 * slots,)),
            dma((2 * slots,)),
            dma,
            dma,
            dma((2,)),
            dma((2,)),
        ],
        compiler_params=pltpu.CompilerParams(
            collective_id=0 if mode == "fast" else 1,
            has_side_effects=True,
            vmem_limit_bytes=40 * 2**20,
        ),
        name="newton_" + mode,
    )(log_rate, shape_rate, events, entry_week, exit_week, log_offset, frailty, kappa_sq)


def per_device(*args):
    both, flag = run("fast", *args)
    both = lax.cond(flag[0] > 0, lambda: both, lambda: run("cg", *args)[0])
    return both[0], both[1]


def solution(mesh):
    tile = P("row", "col")
    return jax.shard_map(
        per_device,
        mesh=mesh,
        in_specs=(P(None, "row", "col"), tile, tile, tile, tile, tile, P(), P()),
        out_specs=(tile, tile),
        check_vma=False,
    )
```

```python
import functools

import jax
import jax.numpy as jnp
from jax import lax
from jax.experimental import pallas as pl
from jax.experimental.pallas import tpu as pltpu
from jax.sharding import PartitionSpec as P


ITERS = 8
TAU = 16.0
MESH = pl.DeviceIdType.MESH
TR, TC = 64, 256
ND = 16
K = 32
GR = 20
EV_PARTS = 4
PIVOT_MIN = 2e-3
W = 2
f32 = jnp.float32


def iota(shape, dim):
    return lax.broadcasted_iota(jnp.int32, shape, dim)


def turn(x, by):
    by = by % 128
    return pltpu.roll(x, by, 1) if by else x


def compose(later, earlier):
    out = {}
    for o, x in later.items():
        for q, y in earlier.items():
            term = x * turn(y, o)
            at = (o + q) % 128
            out[at] = out[at] + term if at in out else term
    return out


def seg_transpose(x):
    sub = iota(x.shape, 0) % 4
    seg = iota(x.shape, 1) // 32
    n = x.shape[0]
    out = x
    for d in (1, 2, 3):
        y = jnp.where(sub + d < 4, pltpu.roll(x, n - d, 0), pltpu.roll(x, 4 - d, 0))
        y = pltpu.roll(y, 32 * d, 1)
        out = jnp.where((seg - sub + 4) % 4 == d, y, out)
    return out


def to_groups(tile_of):
    low = iota((8, 128), 0) < 4
    parts = []
    for t in range(TR // 8):
        a, b = tile_of(t, 0), tile_of(t, 1)
        parts.append(jnp.where(low, a, pltpu.roll(b, 4, 0)))
        parts.append(jnp.where(low, pltpu.roll(a, 4, 0), b))
    return seg_transpose(jnp.concatenate(parts, 0))


def kernel(
    mode,
    lr_hbm,
    sr_hbm,
    ev_hbm,
    en_hbm,
    ex_hbm,
    lo_hbm,
    fr_hbm,
    ka_hbm,
    both_out,
    flag_out,
    lr_ref,
    sr_ref,
    ev,
    en,
    ex,
    lo,
    fr,
    ka,
    e_ref,
    hv_rx,
    hh_tx,
    hh_rx,
    U,
    rx,
    rxv,
    S,
    inv,
    u,
    v,
    pcr,
    Y,
    RHS,
    V,
    RHO,
    AV,
    MK,
    HV,
    GM,
    m1,
    m2,
    g1,
    g2,
    S2,
    OM,
    ORX,
    in_sem,
    hal_send,
    hal_recv,
    rx_send,
    rx_recv,
    rxv_send,
    rxv_recv,
    g_send,
    g_recv,
    o_send,
    o_recv,
    s_send,
    s_recv,
):
    i = lax.axis_index("row")
    j = lax.axis_index("col")
    plane, core = i // 2, i % 2
    m = j % 8
    block = 2 * plane + j // 8
    other = i + 1 - 2 * core
    home = block == i
    up_i, down_i = (i + ND - 1) % ND, (i + 1) % ND
    left_j, right_j = (j + ND - 1) % ND, (j + 1) % ND

    loads = [
        pltpu.make_async_copy(src, dst, in_sem.at[n])
        for n, (src, dst) in enumerate(
            (
                (fr_hbm, fr),
                (ex_hbm, ex),
                (en_hbm, en),
                (lo_hbm, lo),
                (ka_hbm, ka),
                (lr_hbm, lr_ref),
                (sr_hbm, sr_ref),
            )
        )
    ]
    for c in loads:
        c.start()

    barrier = pltpu.get_barrier_semaphore()

    def hello(a, b):
        pl.semaphore_signal(barrier, inc=1, device_id=(a, b), device_id_type=MESH)

    for d in range(1, ND):
        hello(i, (j + d) % ND)
    for d in range(1, ND):
        hello((i + d) % ND, j)
    for d in range(8):
        hello(other, 8 * core + d)

    @pl.when(jnp.logical_not(home))
    def _():
        for b in range(ND):
            hello(other, b)

    ghost_first = (core == 0) & (m == 0)
    ghost_last = (core == 1) & (m == 7)
    ghost_from = (block + jnp.where(core == 0, ND - 1, 1)) % ND
    below_dev = (2 * (down_i // 2), 8 * (down_i % 2))
    above_dev = (2 * (up_i // 2) + 1, 8 * (up_i % 2) + 7)
    below_self = (below_dev[0] == i) & (below_dev[1] == j)
    above_self = (above_dev[0] == i) & (above_dev[1] == j)

    @pl.when(ghost_first | ghost_last)
    def _():
        for b in range(ND):

            @pl.when(jnp.logical_not((ghost_from == i) & (j == b)))
            def _():
                hello(ghost_from, b)

    weeks = ev.shape[0] // EV_PARTS
    ev_loads = [
        pltpu.make_async_copy(
            ev_hbm.at[pl.ds(n * weeks, weeks)], ev.at[pl.ds(n * weeks, weeks)], in_sem.at[7 + n]
        )
        for n in range(EV_PARTS)
    ]
    for c in ev_loads:
        c.start()
    for c in loads:
        c.wait()

    flipped = jnp.concatenate([fr[:, 128:256], fr[:, 0:128]], 0).T
    hh_tx[0] = flipped[120:128]
    hh_tx[1] = flipped[0:8]
    rate = jnp.full((1, TC), sr_ref[0], f32)
    scale = jnp.exp(jnp.full((1, TC), lr_ref[0], f32)) / rate
    slope = rate / float(ev.shape[0])
    exposure = scale * (jnp.exp(slope * ex[...].astype(f32)) - jnp.exp(slope * en[...].astype(f32)))
    weight = exposure * jnp.exp(lo[...] + fr[...])
    e_ref[...] = -weight - TAU * (4.0 + ka[...]) * fr[...]
    diag = 2.0 + ka[...] + weight * (1.0 / TAU)

    fill = iota((2, 8, 128), 0) * 0
    for f, value in ((0, 4.0), (1, 0.0)):
        U[f, 0:2] = fill.astype(f32) + value
        U[f, GR - 2 : GR] = fill.astype(f32) + value
    U[0, 2 : GR - 2] = to_groups(
        lambda t, h: diag[8 * t : 8 * t + 8, 128 * h : 128 * h + 128]
    ).reshape(TR // 4, 8, 128)
    part = diag - 2.0
    part = part[:, 0:128] + part[:, 128:256]
    part = jnp.sum(part, axis=0, keepdims=True)
    m1[0] = jnp.where(iota((W, 128), 0) == 0, part, 0.0)

    def send_field(f):
        for q in (0, 1):
            for d in range(8):
                a = (m + d) % 8
                to = core if q == 0 else 1 - core
                src = U.at[f, pl.ds(2 * a + 3 * to, 3)]

                def start():
                    pltpu.make_async_remote_copy(
                        src_ref=src,
                        dst_ref=rx.at[f, j],
                        send_sem=rx_send.at[f],
                        recv_sem=rx_recv.at[f],
                        device_id=(2 * plane + to, 8 * core + a),
                        device_id_type=MESH,
                    ).start()

                if q == 0 and d == 0:
                    pl.when(jnp.logical_not(home))(start)
                else:
                    start()
        for first, to, here in ((GR - 4, below_dev, below_self), (2, above_dev, above_self)):
            src = U.at[f, pl.ds(first, 2)]

            @pl.when(jnp.logical_not(here))
            def _():
                pltpu.make_async_remote_copy(
                    src_ref=src,
                    dst_ref=rxv.at[f, j],
                    send_sem=rxv_send.at[f],
                    recv_sem=rxv_recv.at[f],
                    device_id=to,
                    device_id_type=MESH,
                ).start()

    def bytes_of(ref, send, recv):
        return pltpu.make_async_remote_copy(
            src_ref=ref,
            dst_ref=ref,
            send_sem=send,
            recv_sem=recv,
            device_id=(i, right_j),
            device_id_type=MESH,
        )

    def one_less(cond, ref, count, send, recv, act):
        @pl.when(cond)
        def _():
            act(bytes_of(ref.at[pl.ds(0, count - 1)], send, recv))

        @pl.when(jnp.logical_not(cond))
        def _():
            act(bytes_of(ref.at[pl.ds(0, count)], send, recv))

    def wait_recv(c):
        c.wait_recv()

    def wait_send(c):
        c.wait_send()

    def group_sends(src, dst, sem, axis):
        if axis == "col":
            me, to = j, [(i, (j + d) % ND) for d in range(1, ND)]
        elif axis == "row":
            me, to = i, [((i + d) % ND, j) for d in range(1, ND)]
        else:
            me, to = plane, [((i + 2 * d) % ND, j) for d in range(1, ND // 2)]
        for dev in to:
            pltpu.make_async_remote_copy(
                src_ref=src,
                dst_ref=dst.at[me],
                send_sem=g_send.at[sem],
                recv_sem=g_recv.at[sem],
                device_id=dev,
                device_id_type=MESH,
            ).start()
        dst[me] = src[...]

    def group_bytes(dst, sem, count):
        return bytes_of(dst.at[pl.ds(0, count - 1)], g_send.at[sem], g_recv.at[sem])

    def exchange(slot):
        group_sends(m1.at[slot], g1.at[slot], 2 * slot, "col")
        group_bytes(g1.at[slot], 2 * slot, ND).wait_recv()
        m2[slot] = jnp.sum(g1[slot], axis=0)
        group_sends(m2.at[slot], g2.at[slot], 2 * slot + 1, "plane")
        group_bytes(g2.at[slot], 2 * slot + 1, ND // 2).wait_recv()
        return jnp.sum(g2[slot, 0 : ND // 2], axis=0)

    greeted = 2 * (ND - 1) + 8 + 2
    greeted = greeted + jnp.where(home, 0, ND)
    greeted = greeted - jnp.where(below_self, 1, 0) - jnp.where(above_self, 1, 0)
    pl.semaphore_wait(barrier, greeted)

    halos = [
        pltpu.make_async_remote_copy(
            src_ref=src,
            dst_ref=dst,
            send_sem=hal_send.at[n],
            recv_sem=hal_recv.at[n],
            device_id=dev,
            device_id_type=MESH,
        )
        for n, (src, dst, dev) in enumerate(
            (
                (fr.at[pl.ds(TR - 8, 8)], hv_rx.at[0], (down_i, j)),
                (fr.at[pl.ds(0, 8)], hv_rx.at[1], (up_i, j)),
                (hh_tx.at[0], hh_rx.at[0], (i, right_j)),
                (hh_tx.at[1], hh_rx.at[1], (i, left_j)),
            )
        )
    ]
    for c in halos:
        c.start()
    send_field(0)
    if mode == "fast":
        group_sends(m1.at[0], g1.at[0], 0, "row")

    en_v, ex_v = en[...], ex[...]
    count = jnp.zeros((TR, TC), jnp.int32)
    for n in range(EV_PARTS):
        ev_loads[n].wait()

        def add_week(w, acc):
            week = w + n * weeks
            at_risk = (week >= en_v) & (week < ex_v)
            return acc + jnp.where(at_risk, ev[week], 0)

        count = lax.fori_loop(0, weeks, add_week, count)
    e_ref[...] = e_ref[...] + count.astype(f32)

    for c in halos:
        c.wait_recv()
    row = iota((TR, 128), 0)
    lane = iota((TR, 128), 1)
    has_up, has_down = jnp.where(i > 0, 1.0, 0.0), jnp.where(i < ND - 1, 1.0, 0.0)
    has_left, has_right = jnp.where(j > 0, 1.0, 0.0), jnp.where(j < ND - 1, 1.0, 0.0)
    lane1 = iota((1, 128), 1)
    edges = jnp.where(lane1 < TR, hh_rx[0, 7:8] * has_left, hh_rx[1, 0:1] * has_right)
    edges = jnp.broadcast_to(edges, (128, 128)).T
    halves = []
    for h in (0, 1):
        cols = slice(128 * h, 128 * h + 128)
        here = fr[:, cols]
        above = jnp.where(row == 0, hv_rx[0, 7:8, cols] * has_up, pltpu.roll(here, 1, 0))
        below = jnp.where(row == TR - 1, hv_rx[1, 0:1, cols] * has_down, pltpu.roll(here, TR - 1, 0))
        there = fr[:, 128 - 128 * h : 256 - 128 * h]
        west_in = edges[0:TR] if h == 0 else pltpu.roll(there, 1, 1)
        east_in = pltpu.roll(there, 127, 1) if h == 0 else edges[TR : 2 * TR]
        west = jnp.where(lane == 0, west_in, pltpu.roll(here, 1, 1))
        east = jnp.where(lane == 127, east_in, pltpu.roll(here, 127, 1))
        total = e_ref[:, cols] + TAU * ((below + above) + (east + west))
        halves.append(total * (1.0 / TAU))
    U[1, 2 : GR - 2] = to_groups(lambda t, h: halves[h][8 * t : 8 * t + 8, :]).reshape(TR // 4, 8, 128)
    send_field(1)

    if mode == "fast":
        group_bytes(g1.at[0], 0, ND).wait_recv()
        m2[0] = jnp.sum(g1[0], axis=0)
        group_sends(m2.at[0], g2.at[0], 1, "col")

    def to_lines(f, dst, outside):
        @pl.when(home)
        def _():
            rx[f, j] = U[f, pl.ds(2 * m + 3 * core, 3)]

        one_less(home, rx.at[f], ND, rx_send.at[f], rx_recv.at[f], wait_recv)

        def ghosts(first, own_first, cond):
            @pl.when(cond)
            def _():
                self_too = ghost_from == i

                @pl.when(self_too)
                def _():
                    rxv[f, j] = U[f, pl.ds(own_first, 2)]

                one_less(self_too, rxv.at[f], ND, rxv_send.at[f], rxv_recv.at[f], wait_recv)
                for b in range(ND):
                    rx[f, b, first : first + 2] = rxv[f, b]

        ghosts(0, GR - 4, ghost_first)
        ghosts(1, 2, ghost_last)
        for g in range(3):
            at = pl.ds(384 * core + 128 * g, 128)
            S[f, at] = rx[f, :, g].reshape(128, 128).T
            pltpu.make_async_remote_copy(
                src_ref=S.at[f, at],
                dst_ref=S.at[f, at],
                send_sem=s_send.at[f],
                recv_sem=s_recv.at[f],
                device_id=(other, j),
                device_id_type=MESH,
            ).start()
        bytes_of(S.at[f, pl.ds(0, 384)], s_send.at[f], s_recv.at[f]).wait_recv()
        inside = MK[...] > 0.5
        for k in range(K):
            lines = jnp.concatenate(
                [S[f, pl.ds(256 * t + k, 8, stride=32), :] for t in range(3)], 0
            )
            dst[k] = jnp.where(inside, lines, outside)

    rows24 = iota((24, 128), 0)
    lanes24 = iota((24, 128), 1)
    lattice_row = 2 * TR * plane + 8 * (j - 1) + rows24
    MK[...] = jnp.where((lattice_row >= 0) & (lattice_row < TR * ND), 1.0, 0.0)

    to_lines(0, Y, 4.0)

    def after(x):
        return jnp.where(lanes24 == 127, 0.0, pltpu.roll(x, 127, 1))

    def before(x):
        return jnp.where(lanes24 == 0, 0.0, pltpu.roll(x, 1, 1))

    p = MK[...] / Y[0]
    inv[0] = p
    prod = p
    u[0] = prod
    for k in range(1, K - 1):
        p = MK[...] / (Y[k] - p)
        inv[k] = p
        prod = prod * p
        u[k] = prod
    last_u = prod
    q = p
    v[K - 2] = q
    w_u = prod
    for k in range(K - 3, -1, -1):
        p_k = inv[k]
        q = p_k * q
        v[k] = q
        w_u = u[k] + p_k * w_u
        u[k] = w_u
    pivot = MK[...] / (Y[K - 1] - p - after(w_u))
    lo_c = jnp.where(lanes24 == 0, 0.0, last_u) * pivot
    hi_c = after(last_u) * pivot
    levels = [{0: pivot}]
    for n in range(7):
        s = 1 << n
        d = 1.0 / (1.0 - lo_c * turn(hi_c, s) - hi_c * turn(lo_c, -s))
        a, b = d * lo_c, d * hi_c
        levels.append({0: d, s: a, 128 - s: b} if n < 6 else {0: d, s: a + b})
        lo_c = a * turn(lo_c, s)
        hi_c = b * turn(hi_c, -s)
    steps = (
        compose(levels[3], compose(levels[2], compose(levels[1], levels[0]))),
        compose(levels[7], compose(levels[6], compose(levels[5], levels[4]))),
    )
    offsets = [sorted(step) for step in steps]
    place = {}
    for n, step in enumerate(steps):
        for o in offsets[n]:
            place[n, o] = len(place)
            pcr[place[n, o]] = step[o]

    to_lines(1, RHS, 0.0)

    def solve(put):
        first = [u[k] * RHS[k] for k in range(4)]
        last = [v[k] * RHS[k] for k in range(4)]
        for k in range(4, K - 1):
            first[k % 4] = first[k % 4] + u[k] * RHS[k]
            last[k % 4] = last[k % 4] + v[k] * RHS[k]
        x = after((first[0] + first[1]) + (first[2] + first[3]))
        x = x + ((last[0] + last[1]) + (last[2] + last[3])) + RHS[K - 1]
        f = inv[0] * RHS[0]
        fs = [f]
        for k in range(1, K - 1):
            f = inv[k] * (RHS[k] + f)
            Y[k] = f
        for n in range(2):
            terms = [pcr[place[n, o]] * turn(x, o) for o in offsets[n]]
            while len(terms) > 1:
                terms = [sum(terms[t : t + 2][1:], terms[t]) for t in range(0, len(terms), 2)]
            x = terms[0]
        for k in range(K - 3, 0, -1):
            f = Y[k] + inv[k] * f
            Y[k] = f
        Y[0] = fs[0] + inv[0] * f
        prev = before(x)
        put(K - 1, x)
        for k in range(K - 2, -1, -1):
            put(k, Y[k] + (u[k] * prev + v[k] * x))

    def across(z):
        return 2.0 * z - (pltpu.roll(z, 1, 0) + pltpu.roll(z, 23, 0))

    own = slice(8, 16)
    sub8 = iota((8, 128), 0)
    lane8 = iota((8, 128), 1)

    if mode == "fast":
        group_bytes(g2.at[0], 1, ND).wait_recv()
        mean = jnp.sum(jnp.sum(g2[0], axis=0), axis=(0, 1), keepdims=True) * (
            1.0 / float(TR * TC * ND * ND)
        )
        HV[...] = jnp.broadcast_to(0.5 * mean, (24, 128))
        zero = jnp.zeros((24, 128), f32)
        for n in (0, 1):
            for k in range(K):
                V[n, k] = zero
                RHO[n, k] = zero[own]

        def basis(it, _):
            w = jnp.where(it == 0, 1.0, HV[...])
            twice = jnp.where(it >= 2, 2.0, 1.0)

            def put(k, x):
                vec = twice * (x * w - V[it + 1, k]) - V[it, k]
                rho = twice * (RHS[k, own] * w[own] - RHO[it + 1, k]) - RHO[it, k]
                V[it + 2, k] = vec
                RHO[it + 2, k] = rho
                tv = across(vec)
                AV[it, k] = rho + tv[own]
                RHS[k] = tv

            solve(put)

            def dots(n, _):
                acc_a = [jnp.zeros((8, 128), f32)] * 4
                acc_n = [jnp.zeros((8, 128), f32)] * 4
                for k in range(K):
                    vec = V[it + 2, k, own]
                    acc_a[k % 4] = acc_a[k % 4] + vec * AV[n, k]
                    acc_n[k % 4] = acc_n[k % 4] + vec * RHO[n + 2, k]
                for first, acc in ((0, acc_a), (64, acc_n)):
                    total = jnp.sum((acc[0] + acc[1]) + (acc[2] + acc[3]), axis=0, keepdims=True)
                    GM[pl.ds(first + 56 - 8 * it + n, 1), :] = total
                    GM[pl.ds(first + 56 - 8 * n + it, 1), :] = total
                return 0

            lax.fori_loop(0, it + 1, dots, 0)
            return 0

        lax.fori_loop(0, ITERS, basis, 0)
        part = jnp.sum(GM[...].T, axis=0, keepdims=True)
        m1[1] = jnp.where(iota((W, 128), 0) == 0, part, 0.0)
        total = exchange(1)
        flat = jnp.sum(total, axis=0, keepdims=True)
        mat = pltpu.roll(jnp.broadcast_to(flat, (8, 128)), 0, 1, stride=8, stride_axis=0)
        worst = jnp.full((8, 1), 1.0, f32)
        diag0 = jnp.sum(jnp.where(lane8 == sub8 + 56, mat, 0.0), axis=1, keepdims=True)
        for n in range(ITERS):
            row_n = jnp.sum(jnp.where(sub8 == n, mat, 0.0), axis=0, keepdims=True)
            col_n = jnp.sum(jnp.where(lane8 == 56 + n, mat, 0.0), axis=1, keepdims=True)
            piv = jnp.sum(jnp.where(sub8[:, 0:1] == n, col_n, 0.0), axis=0, keepdims=True)
            first = jnp.sum(jnp.where(sub8[:, 0:1] == n, diag0, 0.0), axis=0, keepdims=True)
            worst = jnp.minimum(worst, jnp.broadcast_to(piv / first, (8, 1)))
            scaled = row_n / piv
            mat = jnp.where(sub8 == n, jnp.broadcast_to(scaled, (8, 128)), mat - col_n * scaled)
        coef = jnp.sum(jnp.where(lane8 == 120, mat, 0.0), axis=1, keepdims=True)
        coef = jnp.broadcast_to(coef, (8, 128))
        odd = core
        coef = coef * jnp.where(odd == 1, -TAU, 1.0)
        base = jnp.where(odd == 1, TAU, 0.0)
        flag_out[0] = jnp.where(jnp.min(worst) > PIVOT_MIN, 1, 0)
        weights = [jnp.broadcast_to(coef[n : n + 1, :], (8, 128)) for n in range(ITERS)]

        @pl.when(odd == 0)
        def _():
            for k in range(K):
                acc = weights[0] * V[2, k, own]
                for n in range(1, ITERS):
                    acc = acc + weights[n] * V[n + 2, k, own]
                S2[pl.ds(k, 8, stride=32), :] = acc

        @pl.when(odd == 1)
        def _():
            for k in range(K):
                acc = weights[0] * AV[0, k]
                for n in range(1, ITERS):
                    acc = acc + weights[n] * AV[n, k]
                S2[pl.ds(k, 8, stride=32), :] = acc + base * RHO[2, k]

    else:
        zero = jnp.zeros((24, 128), f32)
        for n in (3, 4, 5):
            for k in range(K):
                V[n, k] = zero

        def iterate(it, carry):
            gamma_old, alpha_old = carry
            acc = [jnp.zeros((8, 128), f32)] * 4

            def put(k, x):
                r = RHS[k]
                w = MK[...] * r + across(x)
                V[2, k] = x
                V[6, k] = w
                acc[k % 2] = acc[k % 2] + x[own] * r[own]
                acc[2 + k % 2] = acc[2 + k % 2] + x[own] * w[own]

            solve(put)
            gam = jnp.sum(acc[0] + acc[1], axis=0, keepdims=True)
            mu = jnp.sum(acc[2] + acc[3], axis=0, keepdims=True)
            m1[it] = jnp.where(iota((W, 128), 0) == 0, gam, mu)
            total = jnp.sum(exchange(it), axis=1, keepdims=True)
            gamma = total[0:1]
            mu = total[1:2]
            beta = jnp.where(it == 0, 0.0, gamma / gamma_old)
            alpha = gamma / (mu - beta * gamma / alpha_old)
            for k in range(K):
                p = V[2, k] + beta * V[3, k]
                s = V[6, k] + beta * V[4, k]
                V[3, k] = p
                V[4, k] = s
                V[5, k] = V[5, k] + alpha * p
                RHS[k] = RHS[k] - alpha * s
            return gamma, alpha

        one = jnp.ones((1, 1), f32)
        lax.fori_loop(0, ITERS, iterate, (one, one))
        odd = core
        flag_out[0] = 1

        @pl.when(odd == 0)
        def _():
            for k in range(K):
                S2[pl.ds(k, 8, stride=32), :] = V[5, k, own]

        @pl.when(odd == 1)
        def _():
            for k in range(K):
                S2[pl.ds(k, 8, stride=32), :] = TAU * RHS[k, own]

    for g in range(2):
        OM[:, g] = S2[128 * g : 128 * g + 128].T.reshape(ND, 8, 128)
    slot = 2 * m + core
    for d in range(ND):
        b = (j + d) % ND

        def start():
            pltpu.make_async_remote_copy(
                src_ref=OM.at[b],
                dst_ref=ORX.at[slot],
                send_sem=o_send,
                recv_sem=o_recv,
                device_id=(block, b),
                device_id_type=MESH,
            ).start()

        if d == 0:
            pl.when(jnp.logical_not(home))(start)
        else:
            start()

    @pl.when(home)
    def _():
        ORX[slot] = OM[j]

    one_less(home, ORX, ND, o_send, o_recv, wait_recv)
    low = iota((8, 128), 0) < 4
    for which in (0, 1):
        groups = jnp.concatenate([ORX[2 * t + which, g] for t in range(TR // 8) for g in range(2)], 0)
        groups = seg_transpose(groups)
        for t in range(TR // 8):
            a = groups[16 * t : 16 * t + 8]
            b = groups[16 * t + 8 : 16 * t + 16]
            both_out[which, 8 * t : 8 * t + 8, 0:128] = jnp.where(low, a, pltpu.roll(b, 4, 0))
            both_out[which, 8 * t : 8 * t + 8, 128:256] = jnp.where(low, pltpu.roll(a, 4, 0), b)

    one_less(home, ORX, ND, o_send, o_recv, wait_send)
    for c in halos:
        c.wait_send()
    for f in (0, 1):
        one_less(home, rx.at[f], ND, rx_send.at[f], rx_recv.at[f], wait_send)
        bytes_of(S.at[f, pl.ds(0, 384)], s_send.at[f], s_recv.at[f]).wait_send()
        one_less(
            below_self | above_self, rxv.at[f], 2, rxv_send.at[f], rxv_recv.at[f], wait_send
        )
    for slot in range(2 if mode == "fast" else ITERS):
        first = slot == 0 and mode == "fast"
        group_bytes(g1.at[slot], 2 * slot, ND).wait_send()
        group_bytes(g2.at[slot], 2 * slot + 1, ND if first else ND // 2).wait_send()


def run(mode, events, entry_week, exit_week, log_offset, frailty, kappa_sq, log_rate, shape_rate):
    slots = 2 if mode == "fast" else ITERS
    vm = pltpu.VMEM
    dma = pltpu.SemaphoreType.DMA
    return pl.pallas_call(
        functools.partial(kernel, mode),
        out_shape=(
            jax.ShapeDtypeStruct((2, TR, TC), f32),
            jax.ShapeDtypeStruct((1,), jnp.int32),
        ),
        in_specs=[pl.BlockSpec(memory_space=pltpu.HBM)] * 8,
        out_specs=(
            pl.BlockSpec(memory_space=pltpu.VMEM),
            pl.BlockSpec(memory_space=pltpu.SMEM),
        ),
        scratch_shapes=[
            pltpu.SMEM((1,), f32),
            pltpu.SMEM((1,), f32),
            vm(events.shape, jnp.int32),
            vm((TR, TC), jnp.int32),
            vm((TR, TC), jnp.int32),
            vm((TR, TC), f32),
            vm((TR, TC), f32),
            vm((TR, TC), f32),
            vm((TR, TC), f32),
            vm((2, 8, TC), f32),
            vm((2, 8, 128), f32),
            vm((2, 8, 128), f32),
            vm((2, GR, 8, 128), f32),
            vm((2, ND, 3, 8, 128), f32),
            vm((2, ND, 2, 8, 128), f32),
            vm((2, 800, 128), f32),
            vm((K, 24, 128), f32),
            vm((K, 24, 128), f32),
            vm((K, 24, 128), f32),
            vm((31, 24, 128), f32),
            vm((K, 24, 128), f32),
            vm((K, 24, 128), f32),
            vm((ITERS + 2, K, 24, 128), f32),
            vm((ITERS + 2, K, 8, 128), f32),
            vm((ITERS, K, 8, 128), f32),
            vm((24, 128), f32),
            vm((24, 128), f32),
            vm((128, 128), f32),
            vm((slots, W, 128), f32),
            vm((slots, W, 128), f32),
            vm((slots, ND, W, 128), f32),
            vm((slots, ND, W, 128), f32),
            vm((288, 128), f32),
            vm((ND, 2, 8, 128), f32),
            vm((ND, 2, 8, 128), f32),
            dma((7 + EV_PARTS,)),
            dma((4,)),
            dma((4,)),
            dma((2,)),
            dma((2,)),
            dma((2,)),
            dma((2,)),
            dma((2 * slots,)),
            dma((2 * slots,)),
            dma,
            dma,
            dma((2,)),
            dma((2,)),
        ],
        compiler_params=pltpu.CompilerParams(
            collective_id=0 if mode == "fast" else 1,
            has_side_effects=True,
            vmem_limit_bytes=40 * 2**20,
        ),
        name="newton_" + mode,
    )(log_rate, shape_rate, events, entry_week, exit_week, log_offset, frailty, kappa_sq)


def per_device(*args):
    both, flag = run("fast", *args)
    both = lax.cond(flag[0] > 0, lambda: both, lambda: run("cg", *args)[0])
    return both[0], both[1]


def solution(mesh):
    tile = P("row", "col")
    return jax.shard_map(
        per_device,
        mesh=mesh,
        in_specs=(P(None, "row", "col"), tile, tile, tile, tile, tile, P(), P()),
        out_specs=(tile, tile),
        check_vma=False,
    )
```
